256 devices in a mesh: pipe: 4 (over z_hi, core), dp: 16 (over y, x), tensor: 4 (over z_lo).
Axes of the slice: x: 4, y: 4, z: 8 (z_hi: 2, z_lo: 4; z = z_hi * 4 + z_lo), core: 2. Of those that a mesh axis runs over, the one named last changes fastest.
Arguments:
- section_input: bfloat16 [4, 1, 16, 128, 8192], P('pipe', None, 'dp'), may hold values from -60 to 60
- norm_gain: float32 [4, 8192], P('pipe'), may hold values from 0.1 to 1.9
- key_weight: bfloat16 [4, 8192, 512], P('pipe', None, 'tensor'), may hold values from -0.0625 to 0.0625
- value_weight: bfloat16 [4, 8192, 512], P('pipe', None, 'tensor'), may hold values from -0.0625 to 0.0625
- queries: bfloat16 [4, 1, 16, 128, 4096], P('pipe', None, 'dp', None, 'tensor'), may hold values from -4 to 4
- out_cotangent: bfloat16 [4, 1, 16, 128, 4096], P('pipe', None, 'dp', None, 'tensor'), may hold values from -6 to 6
- segment_ids: int32 [1, 16, 128], P(None, 'dp'), may hold values from 0 to 3, never falling along the last dimension, each value on 1 to 64 neighbouring positions
- upstream: bfloat16 [1, 16, 128, 8192], P(None, 'dp', 'tensor'), may hold values from -2 to 2
Outputs:
- section_cotangent: bfloat16 [4, 1, 16, 128, 8192], P('pipe', None, 'dp', 'tensor')
- query_cotangent: bfloat16 [4, 1, 16, 128, 4096], P('pipe', None, 'dp', None, 'tensor')
- key_weight_grad: float32 [4, 8192, 512], P('pipe', 'dp', 'tensor')
- value_weight_grad: float32 [4, 8192, 512], P('pipe', 'dp', 'tensor')
The draws below stay inside these ranges and needn't reach their ends.
Inputs may be any that keep to these rules, and one draw needn't show every extreme that they name: `segment_ids`: ids never fall along a sequence and start at 0; one document has exactly 64 tokens in every sequence, none more.
All inputs are finite; a program needn't handle non-finite values.
Results may differ from the reference program's by a relative error of at most 0.019.
Values may be sent and summed in bfloat16 or wider, within the bound.
A program may use at most 128 MiB of HBM per device.

```python
import math
import jax
import jax.numpy as jnp
import numpy as np
from jax import lax

D = 8192
HEADS = 32
KV_HEADS = 4
DH = 128
SEQ = 128
MICRO = 1
GROUP = 8
SEQS = 16
N_PIPE = 4


def draw_section_input(key, part):
    key = jax.random.fold_in(key, 11)
    key_base, key_row, key_col = jax.random.split(key, 3)
    array_shape = (N_PIPE, MICRO, SEQS, SEQ, D)
    base_noise = jnp.clip(jax.random.normal(key_base, array_shape, jnp.float32), -6.0, 6.0)
    row_scale = jnp.exp(jax.random.uniform(key_row, (N_PIPE, MICRO, SEQS, SEQ, 1), jnp.float32, 0.0, 2.3))
    col_scale = jnp.exp(jax.random.uniform(key_col, (N_PIPE, 1, 1, 1, D), jnp.float32, 0.0, 2.3))
    return (0.1 * base_noise * row_scale * col_scale).astype(jnp.bfloat16)


def block_levels(stream_key, dims, pieces, low, largest):
    def one(dim, blocks):
        draws = jax.random.uniform(jax.random.fold_in(jax.random.fold_in(stream_key, 6), dim), (blocks,), jnp.float32, low / len(pieces), largest / len(pieces))
        return jnp.repeat(jnp.exp(draws), dims[dim] // blocks).reshape((-1,) + (1,) * (len(dims) - dim - 1))

    level = one(*pieces[0])
    for cut in pieces[1:]:
        level = level * one(*cut)
    return level


def profile(count, total, most, lean):
    weights = [(1 << 20) // math.isqrt(grade ** lean) + 1 for grade in range(2, count + 1)]
    spare, counts = total - most - (count - 1), [1] * (count - 1)
    while spare > 0:
        movable = [i for i in range(count - 1) if counts[i] < most]
        whole, budget = sum([weights[i] for i in movable]), spare
        for i in movable:
            extra = min(most - counts[i], max(1, budget * weights[i] // whole), spare)
            counts[i] = counts[i] + extra
            spare = spare - extra
    return np.array([most] + counts)


def uneven(rng, count, total, limit, lean):
    if count == 2:
        one = jax.random.randint(rng, (), max(1, total - limit), min(limit, total - 1) + 1)
        return jnp.stack([one, total - one])
    tallies = jnp.asarray(profile(count, total, limit, lean), jnp.int32)
    pairs = (count - 1) // 2
    source_of, sink = tallies[1:1 + 2 * pairs:2], tallies[2:2 + 2 * pairs:2]
    slack = jnp.minimum(source_of - 1, limit - sink)
    moved = jax.random.randint(jax.random.fold_in(rng, 1), (pairs,), 0, 1 << 20) % (slack + 1)
    tallies = tallies.at[1:1 + 2 * pairs:2].set(source_of - moved).at[2:2 + 2 * pairs:2].set(sink + moved)
    return tallies[jax.random.permutation(jax.random.fold_in(rng, 2), count)]


def scatter_about(key, extent, scale, limit, cuts=(), dtype=jnp.bfloat16):
    entries = scale * jax.random.normal(key, extent, jnp.float32)
    if cuts:
        entries = entries * block_levels(key, extent, cuts, -0.22, 0.18)
    return jnp.clip(entries, -limit, limit).astype(dtype)


def setup_inputs(seed: int = 0) -> dict:
    seeds = jax.random.split(jax.random.key(seed), 9)
    return {
        "section_input": draw_section_input(jax.random.fold_in(seeds[8], 71), 0),
        "norm_gain": jnp.clip(1.0 + 0.18 * jax.random.normal(seeds[1], (N_PIPE, D), jnp.float32), 0.1, 1.9),
        "key_weight": scatter_about(seeds[2], (N_PIPE, D, KV_HEADS * DH), D ** -0.5, 0.0625, ((0, 4), (2, 4))),
        "value_weight": scatter_about(seeds[3], (N_PIPE, D, KV_HEADS * DH), D ** -0.5, 0.0625, ((0, 4), (2, 4))),
        "queries": scatter_about(seeds[4], (N_PIPE, MICRO, SEQS, SEQ, HEADS * DH), 0.7, 4.0, ((0, 4), (2, 16), (4, 4))),
        "out_cotangent": scatter_about(seeds[5], (N_PIPE, MICRO, SEQS, SEQ, HEADS * DH), 1.0, 6.0, ((0, 4), (2, 16), (4, 4))),
        "segment_ids": jax.vmap(lambda own: jnp.searchsorted(jnp.cumsum(uneven(own, 4, SEQ, SEQ // 2, 0)), jnp.arange(SEQ), side="right"))(jax.random.split(seeds[6], MICRO * SEQS)).reshape((MICRO, SEQS, SEQ)).astype(jnp.int32),
        "upstream": scatter_about(seeds[7], (MICRO, SEQS, SEQ, D), 0.3, 2.0, ((1, 16), (2, 4))),
    }


NORM_EPS = 1e-05

def sequence_grads(inputs, query_rows, cot_rows, seg_row, gain_vec, key_mat, value_mat):
    input_f = inputs.astype(jnp.float32)
    inverse = lax.rsqrt(lax.optimization_barrier(jnp.mean(input_f * input_f, axis=-1, keepdims=True)) + NORM_EPS)
    unit_rows = input_f * inverse
    normed = (unit_rows * gain_vec).astype(jnp.bfloat16)
    keys = jnp.dot(normed, key_mat, preferred_element_type=jnp.float32).astype(jnp.bfloat16)
    values = jnp.dot(normed, value_mat, preferred_element_type=jnp.float32).astype(jnp.bfloat16)
    factor = 1.0 / math.sqrt(DH)
    query_f = query_rows.astype(jnp.float32).reshape(SEQ, KV_HEADS, GROUP, DH)
    cot_f = cot_rows.astype(jnp.float32).reshape(SEQ, KV_HEADS, GROUP, DH)
    key_f = keys.astype(jnp.float32).reshape(SEQ, KV_HEADS, DH)
    value_f = values.astype(jnp.float32).reshape(SEQ, KV_HEADS, DH)
    places = jnp.arange(SEQ)
    allowed = (places[None, :] <= places[:, None]) & (seg_row[:, None] == seg_row[None, :])
    scores = jnp.einsum('ikgd,jkd->kgij', query_f, key_f) * factor
    weights = jnp.where(allowed, jnp.exp(scores), 0.0)
    probs = weights / lax.optimization_barrier(jnp.sum(weights, axis=-1, keepdims=True))
    probs_low = probs.astype(jnp.bfloat16).astype(jnp.float32)
    dprob = jnp.einsum('ikgd,jkd->kgij', cot_f, value_f)
    inner = lax.optimization_barrier(jnp.sum(probs * dprob, axis=-1, keepdims=True))
    dscore = (probs * (dprob - inner)).astype(jnp.bfloat16).astype(jnp.float32)
    query_grad = (jnp.einsum('kgij,jkd->ikgd', dscore, key_f) * factor).astype(jnp.bfloat16)
    key_grad = (jnp.einsum('kgij,ikgd->jkd', dscore, query_f) * factor).astype(jnp.bfloat16)
    value_grad = jnp.einsum('kgij,ikgd->jkd', probs_low, cot_f).astype(jnp.bfloat16)
    key_w3 = key_mat.astype(jnp.float32).reshape(D, KV_HEADS, DH)
    value_w3 = value_mat.astype(jnp.float32).reshape(D, KV_HEADS, DH)
    head_terms = jnp.einsum('jkd,ekd->kje', key_grad.astype(jnp.float32), key_w3)
    head_terms = head_terms + jnp.einsum('jkd,ekd->kje', value_grad.astype(jnp.float32), value_w3)
    head_low = lax.optimization_barrier(head_terms.astype(jnp.bfloat16))
    normed_grad = lax.optimization_barrier(jnp.sum(head_low.astype(jnp.float32), axis=0))
    upper = normed_grad * gain_vec
    contribution = inverse * (upper - unit_rows * lax.optimization_barrier(jnp.mean(upper * unit_rows, axis=-1, keepdims=True)))
    return (contribution, query_grad.reshape(SEQ, HEADS * DH), normed, key_grad.reshape(SEQ, KV_HEADS * DH), value_grad.reshape(SEQ, KV_HEADS * DH))

def section_grads(section_in, gain_vec, key_mat, value_mat, section_queries, section_cots, segment_ids):
    flat_in = section_in.reshape(MICRO * SEQS, SEQ, D)
    flat_queries = section_queries.reshape(MICRO * SEQS, SEQ, HEADS * DH)
    flat_cots = section_cots.reshape(MICRO * SEQS, SEQ, HEADS * DH)
    flat_segs = segment_ids.reshape(MICRO * SEQS, SEQ)

    def one_sequence(items):
        return sequence_grads(items[0], items[1], items[2], items[3], gain_vec, key_mat, value_mat)
    contribution, query_grad, normed, key_grad, value_grad = lax.map(one_sequence, (flat_in, flat_queries, flat_cots, flat_segs))
    normed_flat = normed.reshape(MICRO * SEQS * SEQ, D)
    key_wgrad = jnp.dot(normed_flat.T, key_grad.reshape(MICRO * SEQS * SEQ, KV_HEADS * DH), preferred_element_type=jnp.float32)
    value_wgrad = jnp.dot(normed_flat.T, value_grad.reshape(MICRO * SEQS * SEQ, KV_HEADS * DH), preferred_element_type=jnp.float32)
    return (contribution.reshape(MICRO, SEQS, SEQ, D), query_grad.reshape(MICRO, SEQS, SEQ, HEADS * DH), key_wgrad, value_wgrad)

def reference(section_input, norm_gain, key_weight, value_weight, queries, out_cotangent, segment_ids, upstream):

    def one_section(items):
        return section_grads(items[0], items[1], items[2], items[3], items[4], items[5], segment_ids)
    contributions, query_cotangent, key_weight_grad, value_weight_grad = lax.map(one_section, (section_input, norm_gain, key_weight, value_weight, queries, out_cotangent))
    suffix = jnp.flip(jnp.cumsum(jnp.flip(contributions, 0), axis=0), 0)
    section_cotangent = (upstream.astype(jnp.float32)[None] + suffix).astype(jnp.bfloat16)
    return (section_cotangent, query_cotangent, key_weight_grad, value_weight_grad)
```

```python
import functools
import math

import jax
import jax.numpy as jnp
from jax import lax
from jax.experimental import pallas as pl
from jax.experimental.pallas import tpu as pltpu
from jax.sharding import PartitionSpec as P

NORM_EPS = 1e-05
MESH = pl.DeviceIdType.MESH
F32 = jnp.float32
BF16 = jnp.bfloat16


def kernel(
    dims,
    x_hbm, gain_hbm, kw_hbm, vw_hbm, q_hbm, oc_hbm, seg_hbm, up_hbm,
    sc_out, dq_out, kg_out, vg_out,
    x_v, n_v, w_v, wg_v, q_v, oc_v, seg_v, up_v, gain_v, inv_v,
    nx_v, dq_v, dkv_v, mp_v, mr_v, ag_v, gs_v, gr_v, sr_v, sb_v, so_v,
    ps_v, pr_v, kg_v, vg_v,
    ld, wr, ws_s, ws_r, nx_s, nx_r, zk_s, zk_r, zm_s, zm_r,
    a1_s, a1_r, a2_s, a2_r, g_s, g_r, c_s, c_r, p_s, p_r,
):
    n_pipe, n_dp, n_t, side, seq, width, head, group = dims
    blk = width // n_dp
    quarter = seq // n_t
    two = 2 * head
    pipe = lax.axis_index("pipe")
    d = lax.axis_index("dp")
    t = lax.axis_index("tensor")
    mx = lax.rem(d, side)
    my = d // side

    def at_xy(dx, dy):
        return lax.rem(my + dy, side) * side + lax.rem(mx + dx, side)

    def at_z(dt):
        return lax.rem(t + dt, n_t)

    def local(src, dst, i):
        c = pltpu.make_async_copy(src, dst, ld.at[i])
        c.start()
        return c

    def remote(src, dst, ss, rs, i, dev):
        return pltpu.make_async_remote_copy(
            src_ref=src, dst_ref=dst, send_sem=ss.at[i], recv_sem=rs.at[i],
            device_id=dev, device_id_type=MESH,
        )

    offsets = [(dx, dy) for dy in range(side) for dx in range(side) if dx or dy]

    def dev_d(dd):
        return (pipe, dd, t)

    def dev_t(tt):
        return (pipe, d, tt)

    barrier = pltpu.get_barrier_semaphore()
    for dx, dy in offsets:
        pl.semaphore_signal(barrier, inc=1, device_id=dev_d(at_xy(dx, dy)), device_id_type=MESH)
    for dt in range(1, n_t):
        pl.semaphore_signal(barrier, inc=1, device_id=dev_t(at_z(dt)), device_id_type=MESH)
    for dp_ in range(1, n_pipe):
        pl.semaphore_signal(
            barrier, inc=1, device_id=(lax.rem(pipe + dp_, n_pipe), d, t), device_id_type=MESH
        )

    rows_d = pl.ds(pl.multiple_of(d * blk, blk), blk)
    wcol = pl.multiple_of(t * two, two)
    own_k = local(kw_hbm.at[rows_d], wg_v.at[:, pl.ds(wcol, head)], 0)
    own_v = local(vw_hbm.at[rows_d], wg_v.at[:, pl.ds(wcol + head, head)], 1)
    gain_c = local(gain_hbm, gain_v, 2)

    def rows_of(i):
        return pl.ds(pl.multiple_of(lax.rem(t + i, n_t) * quarter, quarter), quarter)

    x_cs = [local(x_hbm.at[rows_of(i)], x_v.at[rows_of(i)], 3 + i) for i in range(n_t)]
    n_w = 4
    wrows = width // n_w
    w_cs = []
    for i in range(n_w):
        r = pl.ds(i * wrows, wrows)
        w_cs.append(local(kw_hbm.at[r], w_v.at[r, pl.ds(0, head)], 7 + 2 * i))
        w_cs.append(local(vw_hbm.at[r], w_v.at[r, pl.ds(head, head)], 8 + 2 * i))
    seg_c = local(seg_hbm, seg_v, 15)
    q_c = local(q_hbm, q_v, 16)
    oc_c = local(oc_hbm, oc_v, 17)
    up_c = local(up_hbm, up_v, 18)

    step = 512

    def norm_quarter(i):
        r = rows_of(i)
        acc = jnp.zeros((quarter, 128), F32)
        for c in range(0, width, step):
            xf = x_v[r, c:c + step].astype(F32)
            sq = xf * xf
            for j in range(0, step, 128):
                acc = acc + sq[:, j:j + 128]
        mean = jnp.sum(acc, axis=-1, keepdims=True) * (1.0 / width)
        inv = lax.rsqrt(mean + NORM_EPS)
        for c in range(0, width, step):
            xf = x_v[r, c:c + step].astype(F32)
            n_v[r, c:c + step] = (xf * inv * gain_v[:, c:c + step]).astype(BF16)
        return inv

    gain_c.wait()
    x_cs[0].wait()
    inv_v[...] = jnp.broadcast_to(norm_quarter(0), (quarter, 128))
    own_k.wait()
    own_v.wait()
    pl.semaphore_wait(barrier, len(offsets) + n_t - 1 + n_pipe - 1)

    own_rows = rows_of(0)
    w_sends = []
    for dt in range(1, n_t):
        ref = wg_v.at[:, pl.ds(wcol, two)]
        c = remote(ref, ref, ws_s, ws_r, dt - 1, dev_t(at_z(dt)))
        c.start()
        w_sends.append(c)

    def blk_cols(dd):
        return pl.ds(pl.multiple_of(dd * blk, blk), blk)

    n_sends = []
    for i, (dx, dy) in enumerate(offsets):
        dd = at_xy(dx, dy)
        c = remote(n_v.at[own_rows, blk_cols(dd)], nx_v.at[d], nx_s, nx_r, i, dev_d(dd))
        c.start()
        n_sends.append(c)
    nx_v[d] = n_v[own_rows, blk_cols(d)]

    for i in range(1, n_t):
        x_cs[i].wait()
        norm_quarter(i)

    kv = jnp.zeros((seq, two), F32)
    for i in range(n_w):
        w_cs[2 * i].wait()
        w_cs[2 * i + 1].wait()
        kv = kv + jnp.dot(
            n_v[:, i * wrows:(i + 1) * wrows], w_v[i * wrows:(i + 1) * wrows, :],
            preferred_element_type=F32,
        )
    keys = kv[:, :head].astype(BF16)
    values = kv[:, head:].astype(BF16)

    factor = 1.0 / math.sqrt(head)
    seg_c.wait()
    seg_r = jnp.broadcast_to(seg_v[...], (seq, seq))
    ri = lax.broadcasted_iota(jnp.int32, (seq, seq), 0)
    ci = lax.broadcasted_iota(jnp.int32, (seq, seq), 1)
    allowed1 = (ci <= ri) & (seg_r == seg_r.T)
    allowed = jnp.concatenate([allowed1.astype(F32)] * group, axis=0) > 0.5
    q_c.wait()
    oc_c.wait()
    qs = jnp.concatenate([q_v[:, g * head:(g + 1) * head] for g in range(group)], axis=0)
    ocs = jnp.concatenate([oc_v[:, g * head:(g + 1) * head] for g in range(group)], axis=0)
    nt = (((1,), (1,)), ((), ()))
    tn = (((0,), (0,)), ((), ()))
    s = lax.dot_general(qs, keys, nt, preferred_element_type=F32) * factor
    dprob = lax.dot_general(ocs, values, nt, preferred_element_type=F32)
    e = jnp.where(allowed, jnp.exp(s), 0.0)
    probs = e / jnp.sum(e, axis=-1, keepdims=True)
    inner = jnp.sum(probs * dprob, axis=-1, keepdims=True)
    ds_ = (probs * (dprob - inner)).astype(BF16)
    pb = probs.astype(BF16)
    dk = (lax.dot_general(ds_, qs, tn, preferred_element_type=F32) * factor).astype(BF16)
    dv = lax.dot_general(pb, ocs, tn, preferred_element_type=F32).astype(BF16)
    dkv_v[:, :head] = dk
    dkv_v[:, head:] = dv
    msum = jnp.sum(
        dk.astype(F32) * kv[:, :head] + dv.astype(F32) * kv[:, head:], axis=-1, keepdims=True
    )
    mp_v[...] = jnp.broadcast_to(msum, (seq, 128))

    z_sends = []
    for dt in range(1, n_t):
        tt = at_z(dt)
        r = pl.ds(pl.multiple_of(tt * quarter, quarter), quarter)
        c1 = remote(dkv_v.at[r], ag_v.at[my, mx, :, pl.ds(wcol, two)], zk_s, zk_r, dt - 1, dev_t(tt))
        c1.start()
        c2 = remote(mp_v.at[r], mr_v.at[dt], zm_s, zm_r, dt - 1, dev_t(tt))
        c2.start()
        z_sends += [c1, c2]
    ag_v[my, mx, :, pl.ds(wcol, two)] = dkv_v[own_rows, :]
    mr_v[0] = mp_v[own_rows, :]

    dq = (jnp.dot(ds_, keys, preferred_element_type=F32) * factor).astype(BF16)
    for g in range(group):
        dq_v[:, g * head:(g + 1) * head] = dq[g * seq:(g + 1) * seq, :]
    dq_c = pltpu.make_async_copy(dq_v, dq_out, wr.at[0])
    dq_c.start()

    for c in z_sends:
        c.wait()

    half = two * n_t // 2
    p1 = []
    for i in range(1, side):
        ref = ag_v.at[my, mx, :, pl.ds(0, half)]
        c = remote(ref, ref, a1_s, a1_r, i - 1, dev_d(at_xy(i, 0)))
        c.start()
        p1.append(c)
    for i in range(1, side):
        ref = ag_v.at[my, mx, :, pl.ds(half, half)]
        c = remote(ref, ref, a1_s, a1_r, side - 1 + i - 1, dev_d(at_xy(0, i)))
        c.start()
        p1.append(c)
    for c in p1[:side - 1]:
        c.wait()
    p2 = []
    for i in range(1, side):
        ref = ag_v.at[my, :, :, pl.ds(0, half)]
        c = remote(ref, ref, a2_s, a2_r, i - 1, dev_d(at_xy(0, i)))
        c.start()
        p2.append(c)
    for c in p1[side - 1:]:
        c.wait()
    for i in range(1, side):
        ref = ag_v.at[:, mx, :, pl.ds(half, half)]
        c = remote(ref, ref, a2_s, a2_r, side - 1 + i - 1, dev_d(at_xy(i, 0)))
        c.start()
        p2.append(c)

    for c in n_sends:
        c.wait()
    for c in w_sends:
        c.wait()
    nxt = nx_v[...].reshape(n_dp * quarter, blk).T

    for c in p2:
        c.wait()

    g_sends = []
    gi = 0
    for k in range(side):
        yy = lax.rem(my + k, side)
        lhs = ag_v[yy].reshape(side * quarter, n_t * two)
        gk = lax.dot_general(lhs, wg_v[...], nt, preferred_element_type=F32).astype(BF16)
        gs_v[yy] = gk.reshape(side, quarter, blk)
        for dx in range(side):
            if k == 0 and dx == 0:
                continue
            dd = at_xy(dx, k)
            c = remote(
                gs_v.at[yy, lax.rem(mx + dx, side)], gr_v.at[:, blk_cols(d)],
                g_s, g_r, gi, dev_d(dd),
            )
            c.start()
            g_sends.append(c)
            gi += 1
        if k == 0:
            gr_v[:, blk_cols(d)] = gs_v[my, mx]

    full = ag_v[...].reshape(n_dp * quarter, n_t * two)
    part = jnp.dot(nxt, full, preferred_element_type=F32)
    for h in range(n_t):
        ps_v[h] = part[:, h * two:(h + 1) * two].astype(BF16)
    w_red = []
    for dt in range(1, n_t):
        tt = at_z(dt)
        c = remote(ps_v.at[tt], pr_v.at[dt - 1], p_s, p_r, dt - 1, dev_t(tt))
        c.start()
        w_red.append(c)

    up_c.wait()

    @pl.when(pipe == n_pipe - 1)
    def _():
        sr_v[...] = jnp.zeros(sr_v.shape, BF16)

    m = mr_v[0]
    for h in range(1, n_t):
        m = m + mr_v[h]
    m = m[:, :1] * (1.0 / width)
    inv = inv_v[:, :1]
    im = inv * inv * m
    prev = (lax.rem(pipe + n_pipe - 1, n_pipe), d, t)
    cw = side * blk
    outs = []
    chain = []
    gi = 0
    for k in range(side):
        yy = lax.rem(my + side - k, side)
        cols = pl.ds(pl.multiple_of(yy * cw, cw), cw)
        for dx in range(side):
            if k == 0 and dx == 0:
                continue
            g_sends[gi].wait_recv()
            gi += 1
        c = remote(sb_v.at[:, cols], sr_v.at[:, cols], c_s, c_r, k, prev)
        chain.append(c)

        @pl.when(pipe < n_pipe - 1)
        def _():
            c.wait_recv()

        for j in range(0, cw, step):
            cc = pl.ds(pl.multiple_of(yy * cw + j, step), step)
            gf = gr_v[:, cc].astype(F32)
            xf = x_v[own_rows, cc].astype(F32)
            con = inv * (gain_v[:, cc] * gf) - xf * im + sr_v[:, cc].astype(F32)
            sb_v[:, cc] = con.astype(BF16)
            so_v[:, cc] = (up_v[:, cc].astype(F32) + con).astype(BF16)

        @pl.when(pipe > 0)
        def _():
            c.start()

        o = pltpu.make_async_copy(so_v.at[:, cols], sc_out.at[:, cols], wr.at[1 + k])
        o.start()
        outs.append(o)

    for c in w_red:
        c.wait_recv()
    tot = ps_v[t].astype(F32)
    for i in range(n_t - 1):
        tot = tot + pr_v[i].astype(F32)
    kg_v[...] = tot[:, :head]
    vg_v[...] = tot[:, head:]
    kg_c = pltpu.make_async_copy(kg_v, kg_out, wr.at[1 + side])
    vg_c = pltpu.make_async_copy(vg_v, vg_out, wr.at[2 + side])
    kg_c.start()
    vg_c.start()

    for c in p1[:0]:
        c.wait_send()
    for c in g_sends:
        c.wait_send()
    for c in w_red:
        c.wait_send()

    @pl.when(pipe > 0)
    def _():
        for c in chain:
            c.wait_send()

    dq_c.wait()
    for o in outs:
        o.wait()
    kg_c.wait()
    vg_c.wait()


def per_device(sizes, section_input, norm_gain, key_weight, value_weight, queries, out_cotangent,
               segment_ids, upstream):
    n_pipe, n_dp, n_t = sizes
    seq, width = section_input.shape[3:]
    head = key_weight.shape[2]
    group = queries.shape[4] // head
    side = math.isqrt(n_dp)
    blk = width // n_dp
    quarter = seq // n_t
    two = 2 * head
    heads = group * head
    dims = (n_pipe, n_dp, n_t, side, seq, width, head, group)
    V = pltpu.VMEM
    DMA = pltpu.SemaphoreType.DMA
    any_spec = pl.BlockSpec(memory_space=pl.ANY)
    noff = n_dp - 1
    nz = n_t - 1
    na = 2 * (side - 1)
    sc, dq, kg, vg = pl.pallas_call(
        functools.partial(kernel, dims),
        out_shape=(
            jax.ShapeDtypeStruct((quarter, width), BF16),
            jax.ShapeDtypeStruct((seq, heads), BF16),
            jax.ShapeDtypeStruct((blk, head), F32),
            jax.ShapeDtypeStruct((blk, head), F32),
        ),
        in_specs=[any_spec] * 8,
        out_specs=(any_spec,) * 4,
        scratch_shapes=[
            V((seq, width), BF16),
            V((seq, width), BF16),
            V((width, two), BF16),
            V((blk, n_t * two), BF16),
            V((seq, heads), BF16),
            V((seq, heads), BF16),
            V((1, seq), jnp.int32),
            V((quarter, width), BF16),
            V((1, width), F32),
            V((quarter, 128), F32),
            V((n_dp, quarter, blk), BF16),
            V((seq, heads), BF16),
            V((seq, two), BF16),
            V((seq, 128), F32),
            V((n_t, quarter, 128), F32),
            V((side, side, quarter, n_t * two), BF16),
            V((side, side, quarter, blk), BF16),
            V((quarter, width), BF16),
            V((quarter, width), BF16),
            V((quarter, width), BF16),
            V((quarter, width), BF16),
            V((n_t, blk, two), BF16),
            V((nz, blk, two), BF16),
            V((blk, head), F32),
            V((blk, head), F32),
            DMA((19,)), DMA((3 + side,)),
            DMA((nz,)), DMA((nz,)),
            DMA((noff,)), DMA((noff,)),
            DMA((nz,)), DMA((nz,)),
            DMA((nz,)), DMA((nz,)),
            DMA((na,)), DMA((na,)),
            DMA((na,)), DMA((na,)),
            DMA((noff,)), DMA((noff,)),
            DMA((side,)), DMA((side,)),
            DMA((nz,)), DMA((nz,)),
        ],
        compiler_params=pltpu.CompilerParams(
            collective_id=0, has_side_effects=True, vmem_limit_bytes=62 << 20
        ),
        name="attention_backward",
    )(
        section_input.reshape(seq, width),
        norm_gain.reshape(1, width),
        key_weight.reshape(width, head),
        value_weight.reshape(width, head),
        queries.reshape(seq, heads),
        out_cotangent.reshape(seq, heads),
        segment_ids.reshape(1, seq),
        upstream.reshape(quarter, width),
    )
    return (
        sc.reshape(1, 1, 1, quarter, width),
        dq.reshape(1, 1, 1, seq, heads),
        kg[None],
        vg[None],
    )


def solution(mesh):
    sizes = tuple(mesh.shape[a] for a in ("pipe", "dp", "tensor"))
    return jax.shard_map(
        functools.partial(per_device, sizes),
        mesh=mesh,
        in_specs=(
            P("pipe", None, "dp", None, None),
            P("pipe", None),
            P("pipe", None, "tensor"),
            P("pipe", None, "tensor"),
            P("pipe", None, "dp", None, "tensor"),
            P("pipe", None, "dp", None, "tensor"),
            P(None, "dp", None),
            P(None, "dp", "tensor", None),
        ),
        out_specs=(
            P("pipe", None, "dp", "tensor", None),
            P("pipe", None, "dp", None, "tensor"),
            P("pipe", "dp", "tensor"),
            P("pipe", "dp", "tensor"),
        ),
        check_vma=False,
    )
```

```python
import functools
import math

import jax
import jax.numpy as jnp
from jax import lax
from jax.experimental import pallas as pl
from jax.experimental.pallas import tpu as pltpu
from jax.sharding import PartitionSpec as P

NORM_EPS = 1e-05
MESH = pl.DeviceIdType.MESH
F32 = jnp.float32
BF16 = jnp.bfloat16


def far_first(side):
    def hops(o):
        return sum(min(a, side - a) for a in o)

    every = [(dx, dy) for dy in range(side) for dx in range(side) if dx or dy]
    return sorted(every, key=hops, reverse=True)


def kernel(
    dims,
    x_hbm, gain_hbm, kw_hbm, vw_hbm, q_hbm, oc_hbm, seg_hbm, up_hbm,
    sc_out, dq_out, kg_out, vg_out,
    x_v, n_v, w_v, wg_v, q_v, oc_v, seg_v, up_v, gain_v, inv_v,
    nx_v, dq_v, dkv_v, mp_v, mr_v, ag_v, gs_v, gr_v, sr_v, sb_v, so_v,
    ps_v, pr_v, kg_v, vg_v,
    ld, wr, ws_s, ws_r, nx_s, nx_r, zk_s, zk_r, zm_s, zm_r,
    a1_s, a1_r, a2_s, a2_r, g_s, g_r, c_s, c_r, p_s, p_r,
):
    n_pipe, n_dp, n_t, side, seq, width, head, group = dims
    blk = width // n_dp
    quarter = seq // n_t
    two = 2 * head
    pipe = lax.axis_index("pipe")
    d = lax.axis_index("dp")
    t = lax.axis_index("tensor")
    mx = lax.rem(d, side)
    my = d // side

    def at_xy(dx, dy):
        return lax.rem(my + dy, side) * side + lax.rem(mx + dx, side)

    def at_z(dt):
        return lax.rem(t + dt, n_t)

    def local(src, dst, i):
        c = pltpu.make_async_copy(src, dst, ld.at[i])
        c.start()
        return c

    def remote(src, dst, ss, rs, i, dev):
        return pltpu.make_async_remote_copy(
            src_ref=src, dst_ref=dst, send_sem=ss.at[i], recv_sem=rs.at[i],
            device_id=dev, device_id_type=MESH,
        )

    def remote2(src, dst, ss, rs, dev):
        return pltpu.make_async_remote_copy(
            src_ref=src, dst_ref=dst, send_sem=ss, recv_sem=rs,
            device_id=dev, device_id_type=MESH,
        )

    offsets = far_first(side)

    def dev_d(dd):
        return (pipe, dd, t)

    def dev_t(tt):
        return (pipe, d, tt)

    barrier = pltpu.get_barrier_semaphore()
    for dx, dy in offsets:
        pl.semaphore_signal(barrier, inc=1, device_id=dev_d(at_xy(dx, dy)), device_id_type=MESH)
    for dt in range(1, n_t):
        pl.semaphore_signal(barrier, inc=1, device_id=dev_t(at_z(dt)), device_id_type=MESH)
    for dp_ in range(1, n_pipe):
        pl.semaphore_signal(
            barrier, inc=1, device_id=(lax.rem(pipe + dp_, n_pipe), d, t), device_id_type=MESH
        )

    rows_d = pl.ds(pl.multiple_of(d * blk, blk), blk)
    wcol = pl.multiple_of(t * two, two)
    own_k = local(kw_hbm.at[rows_d], wg_v.at[:, pl.ds(wcol, head)], 0)
    own_v = local(vw_hbm.at[rows_d], wg_v.at[:, pl.ds(wcol + head, head)], 1)
    gain_c = local(gain_hbm, gain_v, 2)

    def rows_of(i):
        return pl.ds(pl.multiple_of(lax.rem(t + i, n_t) * quarter, quarter), quarter)

    x_cs = [local(x_hbm.at[rows_of(i)], x_v.at[rows_of(i)], 3 + i) for i in range(n_t)]
    n_w = 4
    wrows = width // n_w
    w_cs = []
    for i in range(n_w):
        r = pl.ds(i * wrows, wrows)
        w_cs.append(local(kw_hbm.at[r], w_v.at[r, pl.ds(0, head)], 7 + 2 * i))
        w_cs.append(local(vw_hbm.at[r], w_v.at[r, pl.ds(head, head)], 8 + 2 * i))
    seg_c = local(seg_hbm, seg_v, 15)
    q_c = local(q_hbm, q_v, 16)
    oc_c = local(oc_hbm, oc_v, 17)
    up_c = local(up_hbm, up_v, 18)

    step = 512

    def norm_quarter(i):
        r = rows_of(i)
        acc = jnp.zeros((quarter, 128), F32)
        for c in range(0, width, step):
            xf = x_v[r, c:c + step].astype(F32)
            sq = xf * xf
            for j in range(0, step, 128):
                acc = acc + sq[:, j:j + 128]
        mean = jnp.sum(acc, axis=-1, keepdims=True) * (1.0 / width)
        inv = lax.rsqrt(mean + NORM_EPS)
        for c in range(0, width, step):
            xf = x_v[r, c:c + step].astype(F32)
            n_v[r, c:c + step] = (xf * inv * gain_v[:, c:c + step]).astype(BF16)
        return inv

    gain_c.wait()
    x_cs[0].wait()
    inv_v[...] = jnp.broadcast_to(norm_quarter(0), (quarter, 128))
    own_k.wait()
    own_v.wait()
    pl.semaphore_wait(barrier, len(offsets) + n_t - 1 + n_pipe - 1)

    own_rows = rows_of(0)
    w_pieces = 4
    prow = blk // w_pieces

    def w_copy(lane, r, q, src, dev):
        cols = pl.ds(pl.multiple_of(src * two, two), two)
        ref = wg_v.at[pl.ds(q * prow, prow), cols]
        return remote(ref, ref, ws_s, ws_r, (r * w_pieces + q) * 2 + lane, dev_t(dev))

    def w_round(r):
        for q in range(w_pieces):
            @pl.when((t - r >= 0) & (t < n_t - 1))
            def _():
                w_copy(0, r, q, t - r, t + 1).start()

            @pl.when((t + r < n_t) & (t > 0))
            def _():
                w_copy(1, r, q, t + r, t - 1).start()

    def w_arrived(r, q):
        @pl.when(t - r - 1 >= 0)
        def _():
            w_copy(0, r, q, t, t).wait_recv()

        @pl.when(t + r + 1 < n_t)
        def _():
            w_copy(1, r, q, t, t).wait_recv()

    def w_sent(r, q):
        @pl.when((t - r >= 0) & (t < n_t - 1))
        def _():
            w_copy(0, r, q, t, t).wait_send()

        @pl.when((t + r < n_t) & (t > 0))
        def _():
            w_copy(1, r, q, t, t).wait_send()

    def w_forward(r):
        for q in range(w_pieces):
            w_arrived(r - 1, q)

            @pl.when((t - r >= 0) & (t < n_t - 1))
            def _():
                w_copy(0, r, q, t - r, t + 1).start()

            @pl.when((t + r < n_t) & (t > 0))
            def _():
                w_copy(1, r, q, t + r, t - 1).start()

    w_round(0)

    def blk_cols(dd):
        return pl.ds(pl.multiple_of(dd * blk, blk), blk)

    n_sends = []
    for i, (dx, dy) in enumerate(offsets):
        dd = at_xy(dx, dy)
        c = remote(n_v.at[own_rows, blk_cols(dd)], nx_v.at[d], nx_s, nx_r, i, dev_d(dd))
        c.start()
        n_sends.append(c)
    nx_v[d] = n_v[own_rows, blk_cols(d)]

    for i in range(1, n_t):
        x_cs[i].wait()
        norm_quarter(i)

    kv = jnp.zeros((seq, two), F32)
    for i in range(n_w):
        w_cs[2 * i].wait()
        w_cs[2 * i + 1].wait()
        kv = kv + jnp.dot(
            n_v[:, i * wrows:(i + 1) * wrows], w_v[i * wrows:(i + 1) * wrows, :],
            preferred_element_type=F32,
        )
    keys = kv[:, :head].astype(BF16)
    values = kv[:, head:].astype(BF16)

    factor = 1.0 / math.sqrt(head)
    seg_c.wait()
    seg_r = jnp.broadcast_to(seg_v[...], (seq, seq))
    ri = lax.broadcasted_iota(jnp.int32, (seq, seq), 0)
    ci = lax.broadcasted_iota(jnp.int32, (seq, seq), 1)
    allowed1 = (ci <= ri) & (seg_r == seg_r.T)
    allowed = jnp.concatenate([allowed1.astype(F32)] * group, axis=0) > 0.5
    q_c.wait()
    oc_c.wait()
    qs = jnp.concatenate([q_v[:, g * head:(g + 1) * head] for g in range(group)], axis=0)
    ocs = jnp.concatenate([oc_v[:, g * head:(g + 1) * head] for g in range(group)], axis=0)
    nt = (((1,), (1,)), ((), ()))
    tn = (((0,), (0,)), ((), ()))
    s = lax.dot_general(qs, keys, nt, preferred_element_type=F32) * factor
    dprob = lax.dot_general(ocs, values, nt, preferred_element_type=F32)
    e = jnp.where(allowed, jnp.exp(s), 0.0)
    probs = e / jnp.sum(e, axis=-1, keepdims=True)
    inner = jnp.sum(probs * dprob, axis=-1, keepdims=True)
    ds_ = (probs * (dprob - inner)).astype(BF16)
    pb = probs.astype(BF16)
    dk = (lax.dot_general(ds_, qs, tn, preferred_element_type=F32) * factor).astype(BF16)
    dv = lax.dot_general(pb, ocs, tn, preferred_element_type=F32).astype(BF16)
    dkv_v[:, :head] = dk
    dkv_v[:, head:] = dv
    msum = jnp.sum(
        dk.astype(F32) * kv[:, :head] + dv.astype(F32) * kv[:, head:], axis=-1, keepdims=True
    )
    mp_v[...] = jnp.broadcast_to(msum, (seq, 128))

    z_sends = []
    for dt in range(1, n_t):
        tt = at_z(dt)
        r = pl.ds(pl.multiple_of(tt * quarter, quarter), quarter)
        c1 = remote(dkv_v.at[r], ag_v.at[my, mx, :, pl.ds(wcol, two)], zk_s, zk_r, dt - 1, dev_t(tt))
        c1.start()
        c2 = remote(mp_v.at[r], mr_v.at[dt], zm_s, zm_r, dt - 1, dev_t(tt))
        c2.start()
        z_sends += [c1, c2]
    ag_v[my, mx, :, pl.ds(wcol, two)] = dkv_v[own_rows, :]
    mr_v[0] = mp_v[own_rows, :]

    w_forward(1)
    for c in z_sends:
        c.wait()

    half = two * n_t // 2

    def piece(h, yy, xx):
        return ag_v.at[yy, xx, :, pl.ds(h * half, half)]

    order = sorted(range(1, side), key=lambda i: -min(i, side - i))
    na = side - 1
    p1 = []
    p2 = []
    for i in order:
        for h in range(2):
            ref = piece(h, my, mx)
            dd = at_xy(i, 0) if h == 0 else at_xy(0, i)
            c = remote(ref, ref, a1_s, a1_r, h * na + i - 1, dev_d(dd))
            c.start()
            p1.append((i, h, c))

    def spread(i, h):
        yy = my if h == 0 else lax.rem(my + side - i, side)
        xx = mx if h == 1 else lax.rem(mx + side - i, side)
        ref = piece(h, yy, xx)
        for j in order:
            dd = at_xy(0, j) if h == 0 else at_xy(j, 0)
            c = remote(ref, ref, a2_s, a2_r, (h * side + i) * na + j - 1, dev_d(dd))
            c.start()
            p2.append(c)

    spread(0, 0)
    spread(0, 1)

    dq = (jnp.dot(ds_, keys, preferred_element_type=F32) * factor).astype(BF16)
    for g in range(group):
        dq_v[:, g * head:(g + 1) * head] = dq[g * seq:(g + 1) * seq, :]
    dq_c = pltpu.make_async_copy(dq_v, dq_out, wr.at[0])
    dq_c.start()

    for i, h, c in p1:
        c.wait_recv()
        spread(i, h)
    w_forward(2)

    for c in n_sends:
        c.wait()
    nxt = nx_v[...].reshape(n_dp * quarter, blk).T

    for i, h, c in p1:
        c.wait_send()
    for c in p2:
        c.wait()

    full = ag_v[...].reshape(n_dp * quarter, n_t * two)
    part = jnp.dot(nxt, full, preferred_element_type=F32)
    for h in range(n_t):
        ps_v[h] = part[:, h * two:(h + 1) * two].astype(BF16)

    def p_copy(term, dev, slot):
        return remote2(ps_v.at[term], pr_v.at[slot], p_s.at[term], p_r.at[slot], dev_t(dev))

    last = n_t - 1

    @pl.when(t == 0)
    def _():
        p_copy(3, 1, 1).start()
        p_copy(2, 2, 0).start()
        p_copy(1, 1, 0).start()
        pr_v[3] = jnp.zeros(pr_v.shape[1:], BF16)

    @pl.when(t == 1)
    def _():
        p_copy(2, 2, 1).start()
        p_copy(0, 0, 1).start()

    @pl.when(t == 2)
    def _():
        p_copy(1, 1, 2).start()
        p_copy(3, 3, 2).start()

    @pl.when(t == last)
    def _():
        p_copy(0, 2, 2).start()
        p_copy(1, 1, 3).start()
        p_copy(2, 2, 3).start()
        pr_v[0] = jnp.zeros(pr_v.shape[1:], BF16)

    for q in range(w_pieces):
        w_arrived(2, q)
    gfull = lax.dot_general(full, wg_v[...], nt, preferred_element_type=F32).astype(BF16)
    gs_v[...] = gfull.reshape(n_dp, quarter, blk)
    g_sends = []
    for i, (dx, dy) in enumerate(offsets):
        dd = at_xy(dx, dy)
        c = remote(gs_v.at[dd], gr_v.at[i], g_s, g_r, i, dev_d(dd))
        c.start()
        g_sends.append(c)
    gr_v[n_dp - 1] = gs_v[d]

    @pl.when(t == 1)
    def _():
        p_copy(3, 1, 1).wait_recv()
        ps_v[3] = (ps_v[3].astype(F32) + pr_v[1].astype(F32)).astype(BF16)
        p_copy(3, 3, 1).start()

    @pl.when(t == 2)
    def _():
        p_copy(0, 2, 2).wait_recv()
        ps_v[0] = (ps_v[0].astype(F32) + pr_v[2].astype(F32)).astype(BF16)
        p_copy(0, 0, 2).start()

    up_c.wait()

    @pl.when(pipe == n_pipe - 1)
    def _():
        sr_v[...] = jnp.zeros(sr_v.shape, BF16)

    m = mr_v[0]
    for h in range(1, n_t):
        m = m + mr_v[h]
    m = m[:, :1] * (1.0 / width)
    inv = inv_v[:, :1]
    im = inv * inv * m
    prev = (lax.rem(pipe + n_pipe - 1, n_pipe), d, t)
    outs = []
    chain = []
    per = n_dp // side
    for k in range(side):
        lo = k * per
        c = remote(sb_v.at[pl.ds(lo, per)], sr_v.at[pl.ds(lo, per)], c_s, c_r, k, prev)
        chain.append(c)
        for i in range(lo, lo + per):
            if i < n_dp - 1:
                g_sends[i].wait_recv()

        @pl.when(pipe < n_pipe - 1)
        def _():
            c.wait_recv()

        for i in range(lo, lo + per):
            dx, dy = offsets[i] if i < n_dp - 1 else (0, 0)
            cc = blk_cols(at_xy(side - dx, side - dy))
            gf = gr_v[i].astype(F32)
            xf = x_v[own_rows, cc].astype(F32)
            con = inv * (gain_v[:, cc] * gf) - xf * im + sr_v[i].astype(F32)
            sb_v[i] = con.astype(BF16)
            so_v[:, cc] = (up_v[:, cc].astype(F32) + con).astype(BF16)

        @pl.when(pipe > 0)
        def _():
            c.start()

    o = pltpu.make_async_copy(so_v, sc_out, wr.at[1])
    o.start()
    outs.append(o)

    for src in range(n_t):
        @pl.when((t != src) & (abs(t - src) < last))
        def _():
            p_copy(0, 0, src).wait_recv()

    tot = ps_v[t].astype(F32)
    for i in range(1, n_t):
        tot = tot + pr_v[at_z(i)].astype(F32)
    kg_v[...] = tot[:, :head]
    vg_v[...] = tot[:, head:]
    kg_c = pltpu.make_async_copy(kg_v, kg_out, wr.at[1 + side])
    vg_c = pltpu.make_async_copy(vg_v, vg_out, wr.at[2 + side])
    kg_c.start()
    vg_c.start()

    for c in g_sends:
        c.wait_send()
    for r in range(n_t - 1):
        for q in range(w_pieces):
            w_sent(r, q)
    for h in range(n_t):
        @pl.when(t != h)
        def _():
            p_copy(h, 0, 0).wait_send()

    @pl.when(pipe > 0)
    def _():
        for c in chain:
            c.wait_send()

    dq_c.wait()
    for o in outs:
        o.wait()
    kg_c.wait()
    vg_c.wait()


def write_out(*refs):
    n = 4
    ins, outs, bufs, sems = refs[:n], refs[n:2 * n], refs[2 * n:3 * n], refs[3 * n]
    loads = [pltpu.make_async_copy(ins[i], bufs[i], sems.at[0, i]) for i in range(n)]
    stores = [pltpu.make_async_copy(bufs[i], outs[i], sems.at[1, i]) for i in range(n)]
    for c in loads:
        c.start()
    for c, o in zip(loads, stores):
        c.wait()
        o.start()
    for o in stores:
        o.wait()


def per_device(sizes, section_input, norm_gain, key_weight, value_weight, queries, out_cotangent,
               segment_ids, upstream):
    n_pipe, n_dp, n_t = sizes
    seq, width = section_input.shape[3:]
    head = key_weight.shape[2]
    group = queries.shape[4] // head
    side = math.isqrt(n_dp)
    blk = width // n_dp
    quarter = seq // n_t
    two = 2 * head
    heads = group * head
    dims = (n_pipe, n_dp, n_t, side, seq, width, head, group)
    V = pltpu.VMEM
    DMA = pltpu.SemaphoreType.DMA
    any_spec = pl.BlockSpec(memory_space=pl.ANY)
    noff = n_dp - 1
    nz = n_t - 1
    na = 2 * (side - 1)
    sc, dq, kg, vg = pl.pallas_call(
        functools.partial(kernel, dims),
        out_shape=(
            jax.ShapeDtypeStruct((quarter, width), BF16),
            jax.ShapeDtypeStruct((seq, heads), BF16),
            jax.ShapeDtypeStruct((blk, head), F32),
            jax.ShapeDtypeStruct((blk, head), F32),
        ),
        in_specs=[any_spec] * 8,
        out_specs=(any_spec,) * 4,
        scratch_shapes=[
            V((seq, width), BF16),
            V((seq, width), BF16),
            V((width, two), BF16),
            V((blk, n_t * two), BF16),
            V((seq, heads), BF16),
            V((seq, heads), BF16),
            V((1, seq), jnp.int32),
            V((quarter, width), BF16),
            V((1, width), F32),
            V((quarter, 128), F32),
            V((n_dp, quarter, blk), BF16),
            V((seq, heads), BF16),
            V((seq, two), BF16),
            V((seq, 128), F32),
            V((n_t, quarter, 128), F32),
            V((side, side, quarter, n_t * two), BF16),
            V((n_dp, quarter, blk), BF16),
            V((n_dp, quarter, blk), BF16),
            V((n_dp, quarter, blk), BF16),
            V((n_dp, quarter, blk), BF16),
            V((quarter, width), BF16),
            V((n_t, blk, two), BF16),
            V((n_t, blk, two), BF16),
            V((blk, head), F32),
            V((blk, head), F32),
            DMA((19,)), DMA((3 + side,)),
            DMA((8 * nz,)), DMA((8 * nz,)),
            DMA((noff,)), DMA((noff,)),
            DMA((nz,)), DMA((nz,)),
            DMA((nz,)), DMA((nz,)),
            DMA((na,)), DMA((na,)),
            DMA((side * na,)), DMA((side * na,)),
            DMA((noff,)), DMA((noff,)),
            DMA((side,)), DMA((side,)),
            DMA((n_t,)), DMA((n_t,)),
        ],
        compiler_params=pltpu.CompilerParams(
            collective_id=0, has_side_effects=True, vmem_limit_bytes=62 << 20
        ),
        name="attention_backward",
    )(
        section_input.reshape(seq, width),
        norm_gain.reshape(1, width),
        key_weight.reshape(width, head),
        value_weight.reshape(width, head),
        queries.reshape(seq, heads),
        out_cotangent.reshape(seq, heads),
        segment_ids.reshape(1, seq),
        upstream.reshape(quarter, width),
    )
    parts = (sc, dq, kg, vg)
    sc, dq, kg, vg = pl.pallas_call(
        write_out,
        out_shape=tuple(jax.ShapeDtypeStruct(a.shape, a.dtype) for a in parts),
        in_specs=[any_spec] * 4,
        out_specs=(any_spec,) * 4,
        scratch_shapes=[V(a.shape, a.dtype) for a in parts] + [DMA((2, 4))],
        compiler_params=pltpu.CompilerParams(vmem_limit_bytes=62 << 20),
        name="write_out",
    )(*parts)
    return (
        sc.reshape(1, 1, 1, quarter, width),
        dq.reshape(1, 1, 1, seq, heads),
        kg[None],
        vg[None],
    )


def solution(mesh):
    sizes = tuple(mesh.shape[a] for a in ("pipe", "dp", "tensor"))
    return jax.shard_map(
        functools.partial(per_device, sizes),
        mesh=mesh,
        in_specs=(
            P("pipe", None, "dp", None, None),
            P("pipe", None),
            P("pipe", None, "tensor"),
            P("pipe", None, "tensor"),
            P("pipe", None, "dp", None, "tensor"),
            P("pipe", None, "dp", None, "tensor"),
            P(None, "dp", None),
            P(None, "dp", "tensor", None),
        ),
        out_specs=(
            P("pipe", None, "dp", "tensor", None),
            P("pipe", None, "dp", None, "tensor"),
            P("pipe", "dp", "tensor"),
            P("pipe", "dp", "tensor"),
        ),
        check_vma=False,
    )
```

```python
import functools
import math

import jax
import jax.numpy as jnp
from jax import lax
from jax.experimental import pallas as pl
from jax.experimental.pallas import tpu as pltpu
from jax.sharding import PartitionSpec as P

NORM_EPS = 1e-05
MESH = pl.DeviceIdType.MESH
F32 = jnp.float32
BF16 = jnp.bfloat16


def far_first(side):
    def hops(o):
        return sum(min(a, side - a) for a in o)

    every = [(dx, dy) for dy in range(side) for dx in range(side) if dx or dy]
    return sorted(every, key=hops, reverse=True)


def kernel(
    dims,
    x_hbm, gain_hbm, kw_hbm, vw_hbm, q_hbm, oc_hbm, seg_hbm, up_hbm,
    sc_out, dq_out, kg_out, vg_out,
    x_v, n_v, w_v, wg_v, q_v, oc_v, seg_v, up_v, gain_v, inv_v,
    nx_v, dq_v, dkv_v, mp_v, mr_v, ag_v, ax_v, cf_v, fr_v, sr_v, sb_v, so_v,
    pw_v, ps_v, pr_v, kg_v, vg_v,
    ld, wr, ws_s, ws_r, nx_s, nx_r, zk_s, zk_r, zm_s, zm_r,
    a1_s, a1_r, a2_s, a2_r, g_s, g_r, c_s, c_r, p_s, p_r,
):
    n_pipe, n_dp, n_t, side, seq, width, head, group = dims
    blk = width // n_dp
    quarter = seq // n_t
    two = 2 * head
    pipe = lax.axis_index("pipe")
    d = lax.axis_index("dp")
    t = lax.axis_index("tensor")
    mx = lax.rem(d, side)
    my = d // side

    def at_xy(dx, dy):
        return lax.rem(my + dy, side) * side + lax.rem(mx + dx, side)

    def at_z(dt):
        return lax.rem(t + dt, n_t)

    def local(src, dst, i):
        c = pltpu.make_async_copy(src, dst, ld.at[i])
        c.start()
        return c

    def remote(src, dst, ss, rs, i, dev):
        return pltpu.make_async_remote_copy(
            src_ref=src, dst_ref=dst, send_sem=ss.at[i], recv_sem=rs.at[i],
            device_id=dev, device_id_type=MESH,
        )

    offsets = far_first(side)

    def dev_d(dd):
        return (pipe, dd, t)

    def dev_t(tt):
        return (pipe, d, tt)

    barrier = pltpu.get_barrier_semaphore()
    for dx, dy in offsets:
        pl.semaphore_signal(barrier, inc=1, device_id=dev_d(at_xy(dx, dy)), device_id_type=MESH)
    for dt in range(1, n_t):
        pl.semaphore_signal(barrier, inc=1, device_id=dev_t(at_z(dt)), device_id_type=MESH)

    @pl.when(pipe < n_pipe - 1)
    def _():
        pl.semaphore_signal(barrier, inc=1, device_id=(pipe + 1, d, t), device_id_type=MESH)

    rows_d = pl.ds(pl.multiple_of(d * blk, blk), blk)
    wcol = pl.multiple_of(t * two, two)
    own_k = local(kw_hbm.at[rows_d], wg_v.at[:, pl.ds(wcol, head)], 0)
    own_v = local(vw_hbm.at[rows_d], wg_v.at[:, pl.ds(wcol + head, head)], 1)
    gain_c = local(gain_hbm, gain_v, 2)

    lo = lax.rem(t, 2)
    hi = t // 2
    partner = t + 1 - 2 * lo
    order_q = (0, 2, 1, 3)

    def rows_of(i):
        return pl.ds(pl.multiple_of(lax.rem(t + i, n_t) * quarter, quarter), quarter)

    x_cs = {i: local(x_hbm.at[rows_of(i)], x_v.at[rows_of(i)], 3 + i) for i in order_q}
    n_w = 4
    wrows = width // n_w
    w_cs = []
    for i in range(n_w):
        r = pl.ds(i * wrows, wrows)
        w_cs.append(local(kw_hbm.at[r], w_v.at[r, pl.ds(0, head)], 7 + 2 * i))
        w_cs.append(local(vw_hbm.at[r], w_v.at[r, pl.ds(head, head)], 8 + 2 * i))
    seg_c = local(seg_hbm, seg_v, 15)
    q_c = local(q_hbm, q_v, 16)
    oc_c = local(oc_hbm, oc_v, 17)
    up_c = local(up_hbm, up_v, 18)

    step = 512

    def norm_quarter(i):
        r = rows_of(i)
        acc = jnp.zeros((quarter, 128), F32)
        for c in range(0, width, step):
            xf = x_v[r, c:c + step].astype(F32)
            sq = xf * xf
            for j in range(0, step, 128):
                acc = acc + sq[:, j:j + 128]
        mean = jnp.sum(acc, axis=-1, keepdims=True) * (1.0 / width)
        inv = lax.rsqrt(mean + NORM_EPS)
        for c in range(0, width, step):
            xf = x_v[r, c:c + step].astype(F32)
            normed = (xf * inv * gain_v[:, c:c + step]).astype(BF16)
            qi = lax.rem(t + i, n_t)
            n_v[qi // 2, lax.rem(qi, 2), :, c:c + step] = normed
        return inv

    gain_c.wait()
    x_cs[0].wait()
    inv_v[...] = jnp.broadcast_to(norm_quarter(0), (quarter, 128))
    x_cs[2].wait()
    norm_quarter(2)
    own_k.wait()
    own_v.wait()
    peers = len(offsets) + n_t - 1

    @pl.when(pipe > 0)
    def _():
        pl.semaphore_wait(barrier, peers + 1)

    @pl.when(pipe == 0)
    def _():
        pl.semaphore_wait(barrier, peers)

    own_rows = rows_of(0)
    w_pieces = 4
    prow = blk // w_pieces

    def w_copy(lane, r, q, src, dev):
        cols = pl.ds(pl.multiple_of(src * two, two), two)
        ref = wg_v.at[pl.ds(q * prow, prow), cols]
        return remote(ref, ref, ws_s, ws_r, (r * w_pieces + q) * 2 + lane, dev_t(dev))

    def w_round(r):
        for q in range(w_pieces):
            @pl.when((t - r >= 0) & (t < n_t - 1))
            def _():
                w_copy(0, r, q, t - r, t + 1).start()

            @pl.when((t + r < n_t) & (t > 0))
            def _():
                w_copy(1, r, q, t + r, t - 1).start()

    def w_arrived(r, q):
        @pl.when(t - r - 1 >= 0)
        def _():
            w_copy(0, r, q, t, t).wait_recv()

        @pl.when(t + r + 1 < n_t)
        def _():
            w_copy(1, r, q, t, t).wait_recv()

    def w_sent(r, q):
        @pl.when((t - r >= 0) & (t < n_t - 1))
        def _():
            w_copy(0, r, q, t, t).wait_send()

        @pl.when((t + r < n_t) & (t > 0))
        def _():
            w_copy(1, r, q, t, t).wait_send()

    def w_forward(r):
        for q in range(w_pieces):
            w_arrived(r - 1, q)

            @pl.when((t - r >= 0) & (t < n_t - 1))
            def _():
                w_copy(0, r, q, t - r, t + 1).start()

            @pl.when((t + r < n_t) & (t > 0))
            def _():
                w_copy(1, r, q, t + r, t - 1).start()

    w_round(0)

    def blk_cols(dd):
        return pl.ds(pl.multiple_of(dd * blk, blk), blk)

    nw = blk // 2

    def part_cols(dd, p):
        return pl.ds(pl.multiple_of(dd * blk + p * nw, nw), nw)

    oth = 1 - hi
    n_sends = []
    for i, (dx, dy) in enumerate(offsets):
        dd = at_xy(dx, dy)
        c = remote(n_v.at[hi, lo, :, blk_cols(dd)], nx_v.at[my, mx, hi], nx_s, nx_r, i, dev_d(dd))
        c.start()
        n_sends.append(c)
    nx_v[my, mx] = n_v[:, lo, :, blk_cols(d)]

    def send_other(p):
        for i, (dx, dy) in enumerate(offsets):
            dd = at_xy(dx, dy)
            c = remote(
                n_v.at[oth, lo, :, part_cols(dd, p)], nx_v.at[my, mx, oth, :, pl.ds(p * nw, nw)],
                nx_s, nx_r, (p + 1) * len(offsets) + i, dev_d(dd),
            )
            c.start()
            n_sends.append(c)

    send_other(0)

    for i in (1, 3):
        x_cs[i].wait()
        norm_quarter(i)

    kv = jnp.zeros((seq, two), F32)
    for i in range(n_w):
        w_cs[2 * i].wait()
        w_cs[2 * i + 1].wait()
        kv = kv + jnp.dot(
            n_v[:, :, :, i * wrows:(i + 1) * wrows].reshape(seq, wrows), w_v[i * wrows:(i + 1) * wrows, :],
            preferred_element_type=F32,
        )
    keys = kv[:, :head].astype(BF16)
    values = kv[:, head:].astype(BF16)

    factor = 1.0 / math.sqrt(head)
    seg_c.wait()
    seg_r = jnp.broadcast_to(seg_v[...], (seq, seq))
    ri = lax.broadcasted_iota(jnp.int32, (seq, seq), 0)
    ci = lax.broadcasted_iota(jnp.int32, (seq, seq), 1)
    allowed1 = (ci <= ri) & (seg_r == seg_r.T)
    allowed = jnp.concatenate([allowed1.astype(F32)] * group, axis=0) > 0.5
    q_c.wait()
    oc_c.wait()
    qs = jnp.concatenate([q_v[:, g * head:(g + 1) * head] for g in range(group)], axis=0)
    ocs = jnp.concatenate([oc_v[:, g * head:(g + 1) * head] for g in range(group)], axis=0)
    nt = (((1,), (1,)), ((), ()))
    tn = (((0,), (0,)), ((), ()))
    s = lax.dot_general(qs, keys, nt, preferred_element_type=F32) * factor
    dprob = lax.dot_general(ocs, values, nt, preferred_element_type=F32)
    e = jnp.where(allowed, jnp.exp(s), 0.0)
    probs = e / jnp.sum(e, axis=-1, keepdims=True)
    inner = jnp.sum(probs * dprob, axis=-1, keepdims=True)
    ds_ = (probs * (dprob - inner)).astype(BF16)
    pb = probs.astype(BF16)
    dk = (lax.dot_general(ds_, qs, tn, preferred_element_type=F32) * factor).astype(BF16)
    dv = lax.dot_general(pb, ocs, tn, preferred_element_type=F32).astype(BF16)
    dkv_v[:, :head] = dk
    dkv_v[:, head:] = dv
    msum = jnp.sum(
        dk.astype(F32) * kv[:, :head] + dv.astype(F32) * kv[:, head:], axis=-1, keepdims=True
    )
    mfull = jnp.broadcast_to(msum, (seq, 128))
    mtop = mfull.astype(BF16)
    mlow = (mfull - mtop.astype(F32)).astype(BF16)
    lane = lax.broadcasted_iota(jnp.int32, (seq, 128), 1)
    mp_v[...] = jnp.where(lane < 64, mtop.astype(F32), mlow.astype(F32)).astype(BF16)

    def head_cols(h):
        return pl.ds(pl.multiple_of(h * two + (h // 2) * 128, 128), two)

    def extra_cols(par):
        return pl.ds(pl.multiple_of(par * two, two), two)

    z_sends = []
    for dt in range(1, n_t):
        tt = at_z(dt)
        r = pl.ds(pl.multiple_of(tt * quarter, quarter), quarter)
        c = remote(dkv_v.at[r], ag_v.at[my, mx, :, head_cols(t)], zk_s, zk_r, dt - 1, dev_t(tt))
        c.start()
        z_sends.append(c)
    r = pl.ds(pl.multiple_of(lax.rem(partner + 2, n_t) * quarter, quarter), quarter)
    c = remote(dkv_v.at[r], ax_v.at[my, mx, :, extra_cols(lo)], zk_s, zk_r, n_t - 1, dev_t(partner))
    c.start()
    z_sends.append(c)
    m_sends = []
    for dt in range(1, n_t):
        tt = at_z(dt)
        r = pl.ds(pl.multiple_of(tt * quarter, quarter), quarter)
        c = remote(mp_v.at[r], mr_v.at[dt], zm_s, zm_r, dt - 1, dev_t(tt))
        c.start()
        m_sends.append(c)
    ag_v[my, mx, :, head_cols(t)] = dkv_v[own_rows, :]
    ax_v[my, mx, :, extra_cols(lo)] = dkv_v[rows_of(2), :]
    mr_v[0] = mp_v[own_rows, :]

    for c in z_sends:
        c.wait()
    for c in m_sends:
        c.wait()

    m = mr_v[0].astype(F32)
    for h in range(1, n_t):
        m = m + mr_v[h].astype(F32)
    m = (m[:, :1] + m[:, 64:65]) * (1.0 / width)
    lane = lax.broadcasted_iota(jnp.int32, (quarter, 128), 1)
    inv_f = inv_v[...]
    both = jnp.where(lane < 64, inv_f, inv_f * m)
    top = both.astype(BF16).astype(F32)
    fine = lax.rem(lane, 64) >= 32
    ag_v[my, mx, :, 2 * two:2 * two + 128] = jnp.where(fine, both - top, top).astype(BF16)

    order = sorted(range(1, side), key=lambda i: -min(i, side - i))
    na = side - 1

    class Gather:
        def __init__(self, buf, ss, rs, cuts):
            self.buf, self.ss, self.rs, self.cuts = buf, ss, rs, cuts
            self.first, self.second = [], []

        def piece(self, h, yy, xx):
            return self.buf.at[yy, xx, :, pl.ds(*self.cuts[h])]

        def send(self, ref, i, h, axis, dst):
            dd = at_xy(i, 0) if axis == 0 else at_xy(0, i)
            c = remote(ref, ref, self.ss, self.rs, dst, dev_d(dd))
            c.start()
            return c

        def begin(self):
            for i in order:
                for h in range(2):
                    ref = self.piece(h, my, mx)
                    self.first.append((i, h, self.send(ref, i, h, h, h * na + i - 1)))
            self.spread(0, 0)
            self.spread(0, 1)

        def spread(self, i, h):
            yy = my if h == 0 else lax.rem(my + side - i, side)
            xx = mx if h == 1 else lax.rem(mx + side - i, side)
            ref = self.piece(h, yy, xx)
            for j in order:
                n = 2 * na + (h * side + i) * na + j - 1
                self.second.append(self.send(ref, j, h, 1 - h, n))

        def forward(self):
            for i, h, c in self.first:
                c.wait_recv()
                self.spread(i, h)

        def finish(self):
            for i, h, c in self.first:
                c.wait_send()
            for c in self.second:
                c.wait()

    cut = 2 * two + 128
    main = Gather(ag_v, a1_s, a1_r, ((0, cut), (cut, 2 * two)))
    extra = Gather(ax_v, a2_s, a2_r, ((0, two), (two, two)))
    main.begin()
    w_forward(1)

    dq = (jnp.dot(ds_, keys, preferred_element_type=F32) * factor).astype(BF16)
    for g in range(group):
        dq_v[:, g * head:(g + 1) * head] = dq[g * seq:(g + 1) * seq, :]
    dq_c = pltpu.make_async_copy(dq_v, dq_out, wr.at[0])
    dq_c.start()

    main.forward()
    w_forward(2)
    for c in n_sends[:len(offsets)]:
        c.wait()
    main.finish()
    extra.begin()
    send_other(1)

    for q in range(w_pieces):
        w_arrived(2, q)
    tokens = n_dp * quarter
    row = side * quarter
    gain_b = gain_v[:, blk_cols(d)]
    gain_r = 1.0 / gain_b
    prev = (lax.rem(pipe + n_pipe - 1, n_pipe), d, t)
    dys = (2, 1, 3, 0)

    def chain_copy(j):
        return remote(sb_v.at[j], sr_v.at[j], c_s, c_r, j, prev)

    def deliver(j):
        dy = dys[j]
        for dx in range(side):
            i = j * side + dx
            if dx or dy:
                deliver_copy(i).start()
            else:
                fr_v[i] = sb_v[j, mx]

    def deliver_copy(i):
        dx, dy = i % side, dys[i // side]
        src = sb_v.at[i // side, lax.rem(mx + dx, side)]
        return remote(src, fr_v.at[i], g_s, g_r, i, dev_d(at_xy(dx, dy)))

    for j, dy in enumerate(dys):
        yy = lax.rem(my + dy, side)
        lhs = ag_v[yy, :, :, :2 * two].reshape(row, 2 * two)
        g = lax.dot_general(lhs, wg_v[:, :2 * two], nt, preferred_element_type=F32)
        lhs = ag_v[yy, :, :, cut:].reshape(row, 2 * two)
        g = g + lax.dot_general(lhs, wg_v[:, 2 * two:], nt, preferred_element_type=F32)
        sc = ag_v[yy, :, :, 2 * two:cut].reshape(row, 128).astype(F32)
        alpha = sc[:, :1] + sc[:, 32:33]
        beta = sc[:, 64:65] + sc[:, 96:97]
        nrm = nx_v[yy, :, hi].reshape(row, blk).astype(F32)
        con = alpha * (gain_b * g) - (beta * nrm) * gain_r
        cf_v[j] = con

        @pl.when(pipe == n_pipe - 1)
        def _():
            sb_v[j] = con.astype(BF16).reshape(side, quarter, blk)
            chain_copy(j).start()
            deliver(j)

    def chain():
        for j in range(side):
            chain_copy(j).wait_recv()
            tot = cf_v[j] + sr_v[j].reshape(row, blk).astype(F32)
            sb_v[j] = tot.astype(BF16).reshape(side, quarter, blk)

            @pl.when(pipe > 0)
            def _():
                chain_copy(j).start()

            deliver(j)

    @pl.when(pipe == n_pipe - 2)
    def _():
        chain()

    extra.forward()

    for c in n_sends[len(offsets):]:
        c.wait()
    extra.finish()
    nxt_own = nx_v[:, :, hi].reshape(tokens, blk).T
    nxt_oth = nx_v[:, :, oth].reshape(tokens, blk).T
    pair_at = pl.multiple_of(hi * (2 * two + 128), 128)
    own_pair = ag_v[:, :, :, pl.ds(pair_at, 2 * two)]
    part = jnp.dot(nxt_own, own_pair.reshape(tokens, 2 * two), preferred_element_type=F32)
    part = part + jnp.dot(
        nxt_oth, ax_v[...].reshape(tokens, 2 * two), preferred_element_type=F32
    )
    for h in range(2):
        pw_v[h] = part[:, h * two:(h + 1) * two]
    ps_v[...] = pw_v[1 - lo].astype(BF16)
    p_c = remote(ps_v, pr_v, p_s, p_r, 0, dev_t(partner))
    p_c.start()

    @pl.when(pipe < n_pipe - 2)
    def _():
        chain()

    up_c.wait()
    for i in range(n_dp):
        dx, dy = i % side, dys[i // side]
        if dx or dy:
            deliver_copy(i).wait_recv()
        cc = blk_cols(at_xy(side - dx, side - dy))
        so_v[:, cc] = (up_v[:, cc].astype(F32) + fr_v[i].astype(F32)).astype(BF16)
    o = pltpu.make_async_copy(so_v, sc_out, wr.at[1])
    o.start()
    outs = [o]

    p_c.wait()
    tot = pw_v[lo] + pr_v[...].astype(F32)
    kg_v[...] = tot[:, :head]
    vg_v[...] = tot[:, head:]
    kg_c = pltpu.make_async_copy(kg_v, kg_out, wr.at[1 + side])
    vg_c = pltpu.make_async_copy(vg_v, vg_out, wr.at[2 + side])
    kg_c.start()
    vg_c.start()

    for i in range(n_dp):
        if i % side or dys[i // side]:
            deliver_copy(i).wait_send()
    for r in range(n_t - 1):
        for q in range(w_pieces):
            w_sent(r, q)

    @pl.when(pipe > 0)
    def _():
        for k in range(4):
            chain_copy(k).wait_send()

    dq_c.wait()
    for o in outs:
        o.wait()
    kg_c.wait()
    vg_c.wait()


def write_out(*refs):
    n = 4
    ins, outs, bufs, sems = refs[:n], refs[n:2 * n], refs[2 * n:3 * n], refs[3 * n]
    loads = [pltpu.make_async_copy(ins[i], bufs[i], sems.at[0, i]) for i in range(n)]
    stores = [pltpu.make_async_copy(bufs[i], outs[i], sems.at[1, i]) for i in range(n)]
    for c in loads:
        c.start()
    for c, o in zip(loads, stores):
        c.wait()
        o.start()
    for o in stores:
        o.wait()


def per_device(sizes, section_input, norm_gain, key_weight, value_weight, queries, out_cotangent,
               segment_ids, upstream):
    n_pipe, n_dp, n_t = sizes
    seq, width = section_input.shape[3:]
    head = key_weight.shape[2]
    group = queries.shape[4] // head
    side = math.isqrt(n_dp)
    blk = width // n_dp
    quarter = seq // n_t
    two = 2 * head
    heads = group * head
    dims = (n_pipe, n_dp, n_t, side, seq, width, head, group)
    V = pltpu.VMEM
    DMA = pltpu.SemaphoreType.DMA
    any_spec = pl.BlockSpec(memory_space=pl.ANY)
    noff = n_dp - 1
    nz = n_t - 1
    na = 2 * (side - 1)
    sc, dq, kg, vg = pl.pallas_call(
        functools.partial(kernel, dims),
        out_shape=(
            jax.ShapeDtypeStruct((quarter, width), BF16),
            jax.ShapeDtypeStruct((seq, heads), BF16),
            jax.ShapeDtypeStruct((blk, head), F32),
            jax.ShapeDtypeStruct((blk, head), F32),
        ),
        in_specs=[any_spec] * 8,
        out_specs=(any_spec,) * 4,
        scratch_shapes=[
            V((seq, width), BF16),
            V((2, 2, quarter, width), BF16),
            V((width, two), BF16),
            V((blk, n_t * two), BF16),
            V((seq, heads), BF16),
            V((seq, heads), BF16),
            V((1, seq), jnp.int32),
            V((quarter, width), BF16),
            V((1, width), F32),
            V((quarter, 128), F32),
            V((side, side, 2, quarter, blk), BF16),
            V((seq, heads), BF16),
            V((seq, two), BF16),
            V((seq, 128), BF16),
            V((n_t, quarter, 128), BF16),
            V((side, side, quarter, n_t * two + 128), BF16),
            V((side, side, quarter, 2 * two), BF16),
            V((side, side * quarter, blk), F32),
            V((n_dp, quarter, blk), BF16),
            V((side, side, quarter, blk), BF16),
            V((side, side, quarter, blk), BF16),
            V((quarter, width), BF16),
            V((2, blk, two), F32),
            V((blk, two), BF16),
            V((blk, two), BF16),
            V((blk, head), F32),
            V((blk, head), F32),
            DMA((19,)), DMA((3 + side,)),
            DMA((8 * nz,)), DMA((8 * nz,)),
            DMA((3 * noff,)), DMA((3 * noff,)),
            DMA((n_t,)), DMA((n_t,)),
            DMA((nz,)), DMA((nz,)),
            DMA((na + side * na,)), DMA((na + side * na,)),
            DMA((na + side * na,)), DMA((na + side * na,)),
            DMA((n_dp,)), DMA((n_dp,)),
            DMA((4,)), DMA((4,)),
            DMA((1,)), DMA((1,)),
        ],
        compiler_params=pltpu.CompilerParams(
            collective_id=0, has_side_effects=True, vmem_limit_bytes=62 << 20
        ),
        name="attention_backward",
    )(
        section_input.reshape(seq, width),
        norm_gain.reshape(1, width),
        key_weight.reshape(width, head),
        value_weight.reshape(width, head),
        queries.reshape(seq, heads),
        out_cotangent.reshape(seq, heads),
        segment_ids.reshape(1, seq),
        upstream.reshape(quarter, width),
    )
    parts = (sc, dq, kg, vg)
    sc, dq, kg, vg = pl.pallas_call(
        write_out,
        out_shape=tuple(jax.ShapeDtypeStruct(a.shape, a.dtype) for a in parts),
        in_specs=[any_spec] * 4,
        out_specs=(any_spec,) * 4,
        scratch_shapes=[V(a.shape, a.dtype) for a in parts] + [DMA((2, 4))],
        compiler_params=pltpu.CompilerParams(vmem_limit_bytes=62 << 20),
        name="write_out",
    )(*parts)
    return (
        sc.reshape(1, 1, 1, quarter, width),
        dq.reshape(1, 1, 1, seq, heads),
        kg[None],
        vg[None],
    )


def solution(mesh):
    sizes = tuple(mesh.shape[a] for a in ("pipe", "dp", "tensor"))
    return jax.shard_map(
        functools.partial(per_device, sizes),
        mesh=mesh,
        in_specs=(
            P("pipe", None, "dp", None, None),
            P("pipe", None),
            P("pipe", None, "tensor"),
            P("pipe", None, "tensor"),
            P("pipe", None, "dp", None, "tensor"),
            P("pipe", None, "dp", None, "tensor"),
            P(None, "dp", None),
            P(None, "dp", "tensor", None),
        ),
        out_specs=(
            P("pipe", None, "dp", "tensor", None),
            P("pipe", None, "dp", None, "tensor"),
            P("pipe", "dp", "tensor"),
            P("pipe", "dp", "tensor"),
        ),
        check_vma=False,
    )
```

```python
import functools
import math

import jax
import jax.numpy as jnp
from jax import lax
from jax.experimental import pallas as pl
from jax.experimental.pallas import tpu as pltpu
from jax.sharding import PartitionSpec as P

NORM_EPS = 1e-05
MESH = pl.DeviceIdType.MESH
F32 = jnp.float32
BF16 = jnp.bfloat16


def far_first(side):
    def hops(o):
        return sum(min(a, side - a) for a in o)

    every = [(dx, dy) for dy in range(side) for dx in range(side) if dx or dy]
    return sorted(every, key=hops, reverse=True)


def kernel(
    dims,
    x_hbm, gain_hbm, kw_hbm, vw_hbm, q_hbm, oc_hbm, seg_hbm, up_hbm,
    sc_out, dq_out, kg_out, vg_out,
    x_v, n_v, w_v, wg_v, q_v, oc_v, seg_v, up_v, gain_v, inv_v,
    nx_v, dkv_v, mp_v, mr_v, ag_v, ax_v, cf_v, fr_v, sr_v, sb_v,
    pw_v, ps_v, pr_v,
    ld, ws_s, ws_r, nx_s, nx_r, zk_s, zk_r, zm_s, zm_r,
    a1_s, a1_r, a2_s, a2_r, g_s, g_r, c_s, c_r, p_s, p_r,
):
    n_pipe, n_dp, n_t, side, seq, width, head, group = dims
    blk = width // n_dp
    quarter = seq // n_t
    two = 2 * head
    pipe = lax.axis_index("pipe")
    d = lax.axis_index("dp")
    t = lax.axis_index("tensor")
    mx = lax.rem(d, side)
    my = d // side

    def at_xy(dx, dy):
        return lax.rem(my + dy, side) * side + lax.rem(mx + dx, side)

    def at_z(dt):
        return lax.rem(t + dt, n_t)

    def local(src, dst, i):
        c = pltpu.make_async_copy(src, dst, ld.at[i])
        c.start()
        return c

    def remote(src, dst, ss, rs, i, dev):
        return pltpu.make_async_remote_copy(
            src_ref=src, dst_ref=dst, send_sem=ss.at[i], recv_sem=rs.at[i],
            device_id=dev, device_id_type=MESH,
        )

    offsets = far_first(side)

    def dev_d(dd):
        return (pipe, dd, t)

    def dev_t(tt):
        return (pipe, d, tt)

    barrier = pltpu.get_barrier_semaphore()
    for dx, dy in offsets:
        pl.semaphore_signal(barrier, inc=1, device_id=dev_d(at_xy(dx, dy)), device_id_type=MESH)
    for dt in range(1, n_t):
        pl.semaphore_signal(barrier, inc=1, device_id=dev_t(at_z(dt)), device_id_type=MESH)

    @pl.when(pipe < n_pipe - 1)
    def _():
        pl.semaphore_signal(barrier, inc=1, device_id=(pipe + 1, d, t), device_id_type=MESH)

    rows_d = pl.ds(pl.multiple_of(d * blk, blk), blk)
    wcol = pl.multiple_of(t * two, two)
    own_k = local(kw_hbm.at[rows_d], wg_v.at[:, pl.ds(wcol, head)], 0)
    own_v = local(vw_hbm.at[rows_d], wg_v.at[:, pl.ds(wcol + head, head)], 1)
    gain_c = local(gain_hbm, gain_v, 2)

    lo = lax.rem(t, 2)
    hi = t // 2
    partner = t + 1 - 2 * lo
    order_q = (0, 2, 1, 3)

    def rows_of(i):
        return pl.ds(pl.multiple_of(lax.rem(t + i, n_t) * quarter, quarter), quarter)

    x_cs = {i: local(x_hbm.at[rows_of(i)], x_v.at[rows_of(i)], 3 + i) for i in order_q}
    n_w = 4
    wrows = width // n_w
    w_cs = []
    for i in range(n_w):
        r = pl.ds(i * wrows, wrows)
        w_cs.append(local(kw_hbm.at[r], w_v.at[r, pl.ds(0, head)], 7 + 2 * i))
        w_cs.append(local(vw_hbm.at[r], w_v.at[r, pl.ds(head, head)], 8 + 2 * i))
    seg_c = local(seg_hbm, seg_v, 15)
    q_c = local(q_hbm, q_v, 16)
    oc_c = local(oc_hbm, oc_v, 17)
    up_c = local(up_hbm, up_v, 18)

    step = 512

    def norm_quarter(i):
        r = rows_of(i)
        acc = jnp.zeros((quarter, 128), F32)
        for c in range(0, width, step):
            xf = x_v[r, c:c + step].astype(F32)
            sq = xf * xf
            for j in range(0, step, 128):
                acc = acc + sq[:, j:j + 128]
        mean = jnp.sum(acc, axis=-1, keepdims=True) * (1.0 / width)
        inv = lax.rsqrt(mean + NORM_EPS)
        for c in range(0, width, step):
            xf = x_v[r, c:c + step].astype(F32)
            normed = (xf * inv * gain_v[:, c:c + step]).astype(BF16)
            qi = lax.rem(t + i, n_t)
            n_v[qi // 2, lax.rem(qi, 2), :, c:c + step] = normed
        return inv

    own_k.wait()
    own_v.wait()
    peers = len(offsets) + n_t - 1

    @pl.when(pipe > 0)
    def _():
        pl.semaphore_wait(barrier, peers + 1)

    @pl.when(pipe == 0)
    def _():
        pl.semaphore_wait(barrier, peers)

    own_rows = rows_of(0)
    w_pieces = 4
    prow = blk // w_pieces

    def w_copy(lane, r, q, src, dev):
        cols = pl.ds(pl.multiple_of(src * two, two), two)
        ref = wg_v.at[pl.ds(q * prow, prow), cols]
        return remote(ref, ref, ws_s, ws_r, (r * w_pieces + q) * 2 + lane, dev_t(dev))

    def w_round(r):
        for q in range(w_pieces):
            @pl.when((t - r >= 0) & (t < n_t - 1))
            def _():
                w_copy(0, r, q, t - r, t + 1).start()

            @pl.when((t + r < n_t) & (t > 0))
            def _():
                w_copy(1, r, q, t + r, t - 1).start()

    def w_arrived(r, q):
        @pl.when(t - r - 1 >= 0)
        def _():
            w_copy(0, r, q, t, t).wait_recv()

        @pl.when(t + r + 1 < n_t)
        def _():
            w_copy(1, r, q, t, t).wait_recv()

    def w_sent(r, q):
        @pl.when((t - r >= 0) & (t < n_t - 1))
        def _():
            w_copy(0, r, q, t, t).wait_send()

        @pl.when((t + r < n_t) & (t > 0))
        def _():
            w_copy(1, r, q, t, t).wait_send()

    def w_forward(r):
        for q in range(w_pieces):
            w_arrived(r - 1, q)

            @pl.when((t - r >= 0) & (t < n_t - 1))
            def _():
                w_copy(0, r, q, t - r, t + 1).start()

            @pl.when((t + r < n_t) & (t > 0))
            def _():
                w_copy(1, r, q, t + r, t - 1).start()

    w_round(0)

    gain_c.wait()
    x_cs[0].wait()
    inv_v[...] = jnp.broadcast_to(norm_quarter(0), (quarter, 128))
    x_cs[2].wait()
    norm_quarter(2)

    def blk_cols(dd):
        return pl.ds(pl.multiple_of(dd * blk, blk), blk)

    nw = blk // 2

    def part_cols(dd, p):
        return pl.ds(pl.multiple_of(dd * blk + p * nw, nw), nw)

    oth = 1 - hi
    n_sends = []
    for i, (dx, dy) in enumerate(offsets):
        dd = at_xy(dx, dy)
        c = remote(n_v.at[hi, lo, :, blk_cols(dd)], nx_v.at[my, mx, hi], nx_s, nx_r, i, dev_d(dd))
        c.start()
        n_sends.append(c)
    nx_v[my, mx] = n_v[:, lo, :, blk_cols(d)]

    def others(p):
        for i, (dx, dy) in enumerate(offsets):
            dd = at_xy(dx, dy)
            yield remote(
                n_v.at[oth, lo, :, part_cols(dd, p)], nx_v.at[my, mx, oth, :, pl.ds(p * nw, nw)],
                nx_s, nx_r, (p + 1) * len(offsets) + i, dev_d(dd),
            )

    def send_other(p):
        for c in others(p):
            c.start()

    send_other(0)

    for i in (1, 3):
        x_cs[i].wait()
        norm_quarter(i)

    kv = jnp.zeros((seq, two), F32)
    for i in range(n_w):
        w_cs[2 * i].wait()
        w_cs[2 * i + 1].wait()
        kv = kv + jnp.dot(
            n_v[:, :, :, i * wrows:(i + 1) * wrows].reshape(seq, wrows), w_v[i * wrows:(i + 1) * wrows, :],
            preferred_element_type=F32,
        )
    keys = kv[:, :head].astype(BF16)
    values = kv[:, head:].astype(BF16)

    factor = 1.0 / math.sqrt(head)
    seg_c.wait()
    seg_r = jnp.broadcast_to(seg_v[...], (seq, seq))
    ri = lax.broadcasted_iota(jnp.int32, (seq, seq), 0)
    ci = lax.broadcasted_iota(jnp.int32, (seq, seq), 1)
    allowed1 = (ci <= ri) & (seg_r == seg_r.T)
    allowed = jnp.concatenate([allowed1.astype(F32)] * group, axis=0) > 0.5
    q_c.wait()
    oc_c.wait()
    qs = jnp.concatenate([q_v[:, g * head:(g + 1) * head] for g in range(group)], axis=0)
    ocs = jnp.concatenate([oc_v[:, g * head:(g + 1) * head] for g in range(group)], axis=0)
    nt = (((1,), (1,)), ((), ()))
    tn = (((0,), (0,)), ((), ()))
    s = lax.dot_general(qs, keys, nt, preferred_element_type=F32) * factor
    dprob = lax.dot_general(ocs, values, nt, preferred_element_type=F32)
    e = jnp.where(allowed, jnp.exp(s), 0.0)
    probs = e / jnp.sum(e, axis=-1, keepdims=True)
    inner = jnp.sum(probs * dprob, axis=-1, keepdims=True)
    ds_ = (probs * (dprob - inner)).astype(BF16)
    pb = probs.astype(BF16)
    dk = (lax.dot_general(ds_, qs, tn, preferred_element_type=F32) * factor).astype(BF16)
    dv = lax.dot_general(pb, ocs, tn, preferred_element_type=F32).astype(BF16)
    dkv_v[:, :head] = dk
    dkv_v[:, head:] = dv
    msum = jnp.sum(
        dk.astype(F32) * kv[:, :head] + dv.astype(F32) * kv[:, head:], axis=-1, keepdims=True
    )
    mfull = jnp.broadcast_to(msum, (seq, 128))
    mtop = mfull.astype(BF16)
    mlow = (mfull - mtop.astype(F32)).astype(BF16)
    lane = lax.broadcasted_iota(jnp.int32, (seq, 128), 1)
    mp_v[...] = jnp.where(lane < 64, mtop.astype(F32), mlow.astype(F32)).astype(BF16)

    def head_cols(h):
        return pl.ds(pl.multiple_of(h * two + (h // 2) * 128, 128), two)

    def extra_cols(par):
        return pl.ds(pl.multiple_of(par * two, two), two)

    z_sends = []
    for dt in range(1, n_t):
        tt = at_z(dt)
        r = pl.ds(pl.multiple_of(tt * quarter, quarter), quarter)
        c = remote(dkv_v.at[r], ag_v.at[my, mx, :, head_cols(t)], zk_s, zk_r, dt - 1, dev_t(tt))
        c.start()
        z_sends.append(c)
    r = pl.ds(pl.multiple_of(lax.rem(partner + 2, n_t) * quarter, quarter), quarter)
    c = remote(dkv_v.at[r], ax_v.at[my, mx, :, extra_cols(lo)], zk_s, zk_r, n_t - 1, dev_t(partner))
    c.start()
    z_sends.append(c)
    m_sends = []
    for dt in range(1, n_t):
        tt = at_z(dt)
        r = pl.ds(pl.multiple_of(tt * quarter, quarter), quarter)
        c = remote(mp_v.at[r], mr_v.at[dt], zm_s, zm_r, dt - 1, dev_t(tt))
        c.start()
        m_sends.append(c)
    ag_v[my, mx, :, head_cols(t)] = dkv_v[own_rows, :]
    ax_v[my, mx, :, extra_cols(lo)] = dkv_v[rows_of(2), :]
    mr_v[0] = mp_v[own_rows, :]

    for c in z_sends:
        c.wait()
    for c in m_sends:
        c.wait()

    m = mr_v[0].astype(F32)
    for h in range(1, n_t):
        m = m + mr_v[h].astype(F32)
    m = (m[:, :1] + m[:, 64:65]) * (1.0 / width)
    lane = lax.broadcasted_iota(jnp.int32, (quarter, 128), 1)
    inv_f = inv_v[...]
    both = jnp.where(lane < 64, inv_f, inv_f * m)
    top = both.astype(BF16).astype(F32)
    fine = lax.rem(lane, 64) >= 32
    ag_v[my, mx, :, 2 * two:2 * two + 128] = jnp.where(fine, both - top, top).astype(BF16)

    order = sorted(range(1, side), key=lambda i: -min(i, side - i))
    na = side - 1

    class Gather:
        def __init__(self, buf, ss, rs, cuts):
            self.buf, self.ss, self.rs, self.cuts = buf, ss, rs, cuts

        def piece(self, h, yy, xx):
            return self.buf.at[yy, xx, :, pl.ds(*self.cuts[h])]

        def copy(self, ref, i, axis, n):
            dd = at_xy(i, 0) if axis == 0 else at_xy(0, i)
            return remote(ref, ref, self.ss, self.rs, n, dev_d(dd))

        def first(self, i, h):
            return self.copy(self.piece(h, my, mx), i, h, h * na + i - 1)

        def second(self, i, h, j):
            yy = my if h == 0 else lax.rem(my + side - i, side)
            xx = mx if h == 1 else lax.rem(mx + side - i, side)
            n = 2 * na + (h * side + i) * na + j - 1
            return self.copy(self.piece(h, yy, xx), j, 1 - h, n)

        def begin(self):
            for i in order:
                for h in range(2):
                    self.first(i, h).start()
            self.spread(0, 0)
            self.spread(0, 1)

        def spread(self, i, h):
            for j in order:
                self.second(i, h, j).start()

        def forward(self):
            for i in order:
                for h in range(2):
                    self.first(i, h).wait_recv()
                    self.spread(i, h)

        def finish(self):
            for i in order:
                for h in range(2):
                    self.first(i, h).wait_send()
            for i in range(side):
                for h in range(2):
                    for j in order:
                        self.second(i, h, j).wait()

    cut = 2 * two + 128
    main = Gather(ag_v, a1_s, a1_r, ((0, cut), (cut, 2 * two)))
    extra = Gather(ax_v, a2_s, a2_r, ((0, two), (two, two)))
    main.begin()
    w_forward(1)

    dq = (jnp.dot(ds_, keys, preferred_element_type=F32) * factor).astype(BF16)
    for g in range(group):
        dq_out[:, g * head:(g + 1) * head] = dq[g * seq:(g + 1) * seq, :]

    main.forward()
    w_forward(2)
    for c in n_sends:
        c.wait()
    main.finish()
    @pl.when(pipe < n_pipe - 2)
    def _():
        extra.begin()
        send_other(1)


    for q in range(w_pieces):
        w_arrived(2, q)
    tokens = n_dp * quarter
    row = side * quarter
    gain_b = gain_v[:, blk_cols(d)]
    gain_r = 1.0 / gain_b
    prev = (lax.rem(pipe + n_pipe - 1, n_pipe), d, t)
    dys = (2, 1, 3, 0)

    def chain_copy(j):
        return remote(sb_v.at[j], sr_v.at[j], c_s, c_r, j, prev)

    def deliver(j):
        dy = dys[j]
        for dx in range(side):
            i = j * side + dx
            if dx or dy:
                deliver_copy(i).start()
            else:
                fr_v[i] = sb_v[j, mx]

    def deliver_copy(i):
        dx, dy = i % side, dys[i // side]
        src = sb_v.at[i // side, lax.rem(mx + dx, side)]
        return remote(src, fr_v.at[i], g_s, g_r, i, dev_d(at_xy(dx, dy)))

    for j, dy in enumerate(dys):
        yy = lax.rem(my + dy, side)
        lhs = ag_v[yy, :, :, :2 * two].reshape(row, 2 * two)
        g = lax.dot_general(lhs, wg_v[:, :2 * two], nt, preferred_element_type=F32)
        lhs = ag_v[yy, :, :, cut:].reshape(row, 2 * two)
        g = g + lax.dot_general(lhs, wg_v[:, 2 * two:], nt, preferred_element_type=F32)
        sc = ag_v[yy, :, :, 2 * two:cut].reshape(row, 128).astype(F32)
        alpha = sc[:, :1] + sc[:, 32:33]
        beta = sc[:, 64:65] + sc[:, 96:97]
        nrm = nx_v[yy, :, hi].reshape(row, blk).astype(F32)
        con = alpha * (gain_b * g) - (beta * nrm) * gain_r
        cf_v[j] = con

        @pl.when(pipe == n_pipe - 1)
        def _():
            sb_v[j] = con.astype(BF16).reshape(side, quarter, blk)
            chain_copy(j).start()
            deliver(j)

    def chain():
        for j in range(side):
            chain_copy(j).wait_recv()
            tot = cf_v[j] + sr_v[j].reshape(row, blk).astype(F32)
            sb_v[j] = tot.astype(BF16).reshape(side, quarter, blk)

            @pl.when(pipe > 0)
            def _():
                chain_copy(j).start()

            deliver(j)

    @pl.when(pipe == n_pipe - 2)
    def _():
        chain()

    @pl.when(pipe >= n_pipe - 2)
    def _():
        extra.begin()
        send_other(1)

    extra.forward()

    for p in range(2):
        for c in others(p):
            c.wait()
    extra.finish()
    nxt_own = nx_v[:, :, hi].reshape(tokens, blk).T
    nxt_oth = nx_v[:, :, oth].reshape(tokens, blk).T
    pair_at = pl.multiple_of(hi * (2 * two + 128), 128)
    own_pair = ag_v[:, :, :, pl.ds(pair_at, 2 * two)]
    part = jnp.dot(nxt_own, own_pair.reshape(tokens, 2 * two), preferred_element_type=F32)
    part = part + jnp.dot(
        nxt_oth, ax_v[...].reshape(tokens, 2 * two), preferred_element_type=F32
    )
    for h in range(2):
        pw_v[h] = part[:, h * two:(h + 1) * two]
    ps_v[...] = pw_v[1 - lo].astype(BF16)
    p_c = remote(ps_v, pr_v, p_s, p_r, 0, dev_t(partner))
    p_c.start()

    @pl.when(pipe < n_pipe - 2)
    def _():
        chain()

    up_c.wait()
    for i in range(n_dp):
        dx, dy = i % side, dys[i // side]
        if dx or dy:
            deliver_copy(i).wait_recv()
        cc = blk_cols(at_xy(side - dx, side - dy))
        sc_out[:, cc] = (up_v[:, cc].astype(F32) + fr_v[i].astype(F32)).astype(BF16)

    p_c.wait()
    tot = pw_v[lo] + pr_v[...].astype(F32)
    kg_out[...] = tot[:, :head]
    vg_out[...] = tot[:, head:]
    for i in range(n_dp):
        if i % side or dys[i // side]:
            deliver_copy(i).wait_send()
    for r in range(n_t - 1):
        for q in range(w_pieces):
            w_sent(r, q)

    @pl.when(pipe > 0)
    def _():
        for k in range(4):
            chain_copy(k).wait_send()


def write_out(*refs):
    n = 4
    ins, outs, sems = refs[:n], refs[n:2 * n], refs[2 * n]
    stores = [pltpu.make_async_copy(ins[i], outs[i], sems.at[i]) for i in range(n)]
    for o in stores:
        o.start()
    for o in stores:
        o.wait()


def per_device(sizes, section_input, norm_gain, key_weight, value_weight, queries, out_cotangent,
               segment_ids, upstream):
    n_pipe, n_dp, n_t = sizes
    seq, width = section_input.shape[3:]
    head = key_weight.shape[2]
    group = queries.shape[4] // head
    side = math.isqrt(n_dp)
    blk = width // n_dp
    quarter = seq // n_t
    two = 2 * head
    heads = group * head
    dims = (n_pipe, n_dp, n_t, side, seq, width, head, group)
    V = pltpu.VMEM
    DMA = pltpu.SemaphoreType.DMA
    any_spec = pl.BlockSpec(memory_space=pl.ANY)
    noff = n_dp - 1
    nz = n_t - 1
    na = 2 * (side - 1)
    sc, dq, kg, vg = pl.pallas_call(
        functools.partial(kernel, dims),
        out_shape=(
            V((quarter, width), BF16),
            V((seq, heads), BF16),
            V((blk, head), F32),
            V((blk, head), F32),
        ),
        in_specs=[any_spec] * 8,
        out_specs=(pl.BlockSpec(memory_space=V),) * 4,
        scratch_shapes=[
            V((seq, width), BF16),
            V((2, 2, quarter, width), BF16),
            V((width, two), BF16),
            V((blk, n_t * two), BF16),
            V((seq, heads), BF16),
            V((seq, heads), BF16),
            V((1, seq), jnp.int32),
            V((quarter, width), BF16),
            V((1, width), F32),
            V((quarter, 128), F32),
            V((side, side, 2, quarter, blk), BF16),
            V((seq, two), BF16),
            V((seq, 128), BF16),
            V((n_t, quarter, 128), BF16),
            V((side, side, quarter, n_t * two + 128), BF16),
            V((side, side, quarter, 2 * two), BF16),
            V((side, side * quarter, blk), F32),
            V((n_dp, quarter, blk), BF16),
            V((side, side, quarter, blk), BF16),
            V((side, side, quarter, blk), BF16),
            V((2, blk, two), F32),
            V((blk, two), BF16),
            V((blk, two), BF16),
            DMA((19,)),
            DMA((8 * nz,)), DMA((8 * nz,)),
            DMA((3 * noff,)), DMA((3 * noff,)),
            DMA((n_t,)), DMA((n_t,)),
            DMA((nz,)), DMA((nz,)),
            DMA((na + side * na,)), DMA((na + side * na,)),
            DMA((na + side * na,)), DMA((na + side * na,)),
            DMA((n_dp,)), DMA((n_dp,)),
            DMA((4,)), DMA((4,)),
            DMA((1,)), DMA((1,)),
        ],
        compiler_params=pltpu.CompilerParams(
            collective_id=0, has_side_effects=True, vmem_limit_bytes=62 << 20
        ),
        name="attention_backward",
    )(
        section_input.reshape(seq, width),
        norm_gain.reshape(1, width),
        key_weight.reshape(width, head),
        value_weight.reshape(width, head),
        queries.reshape(seq, heads),
        out_cotangent.reshape(seq, heads),
        segment_ids.reshape(1, seq),
        upstream.reshape(quarter, width),
    )
    parts = (sc, dq, kg, vg)
    sc, dq, kg, vg = pl.pallas_call(
        write_out,
        out_shape=tuple(jax.ShapeDtypeStruct(a.shape, a.dtype) for a in parts),
        in_specs=[pl.BlockSpec(memory_space=V)] * 4,
        out_specs=(any_spec,) * 4,
        scratch_shapes=[DMA((4,))],
        compiler_params=pltpu.CompilerParams(vmem_limit_bytes=16 << 20),
        name="write_out",
    )(*parts)
    return (
        sc.reshape(1, 1, 1, quarter, width),
        dq.reshape(1, 1, 1, seq, heads),
        kg[None],
        vg[None],
    )


def solution(mesh):
    sizes = tuple(mesh.shape[a] for a in ("pipe", "dp", "tensor"))
    return jax.shard_map(
        functools.partial(per_device, sizes),
        mesh=mesh,
        in_specs=(
            P("pipe", None, "dp", None, None),
            P("pipe", None),
            P("pipe", None, "tensor"),
            P("pipe", None, "tensor"),
            P("pipe", None, "dp", None, "tensor"),
            P("pipe", None, "dp", None, "tensor"),
            P(None, "dp", None),
            P(None, "dp", "tensor", None),
        ),
        out_specs=(
            P("pipe", None, "dp", "tensor", None),
            P("pipe", None, "dp", None, "tensor"),
            P("pipe", "dp", "tensor"),
            P("pipe", "dp", "tensor"),
        ),
        check_vma=False,
    )
```

```python
import functools
import math

import jax
import jax.numpy as jnp
from jax import lax
from jax.experimental import pallas as pl
from jax.experimental.pallas import tpu as pltpu
from jax.sharding import PartitionSpec as P

NORM_EPS = 1e-05
MESH = pl.DeviceIdType.MESH
F32 = jnp.float32
BF16 = jnp.bfloat16


def far_first(side):
    def hops(o):
        return sum(min(a, side - a) for a in o)

    every = [(dx, dy) for dy in range(side) for dx in range(side) if dx or dy]
    return sorted(every, key=hops, reverse=True)


def kernel(
    dims,
    x_hbm, gain_hbm, kw_hbm, vw_hbm, q_hbm, oc_hbm, seg_hbm, up_hbm,
    sc_out, dq_out, kg_out, vg_out,
    x_v, n_v, w_v, wg_v, q_v, oc_v, seg_v, up_v, gain_v, inv_v,
    nx_v, dkv_v, mp_v, mr_v, ag_v, ax_v, cf_v, fr_v, sr_v, sb_v,
    pw_v, ps_v, pr_v,
    ld, ws_s, ws_r, nx_s, nx_r, zk_s, zk_r, zm_s, zm_r,
    a1_s, a1_r, a2_s, a2_r, g_s, g_r, c_s, c_r, p_s, p_r,
):
    n_pipe, n_dp, n_t, side, seq, width, head, group = dims
    blk = width // n_dp
    quarter = seq // n_t
    two = 2 * head
    pipe = lax.axis_index("pipe")
    d = lax.axis_index("dp")
    t = lax.axis_index("tensor")
    mx = lax.rem(d, side)
    my = d // side

    def at_xy(dx, dy):
        return lax.rem(my + dy, side) * side + lax.rem(mx + dx, side)

    def at_z(dt):
        return lax.rem(t + dt, n_t)

    def local(src, dst, i):
        c = pltpu.make_async_copy(src, dst, ld.at[i])
        c.start()
        return c

    def remote(src, dst, ss, rs, i, dev):
        return pltpu.make_async_remote_copy(
            src_ref=src, dst_ref=dst, send_sem=ss.at[i], recv_sem=rs.at[i],
            device_id=dev, device_id_type=MESH,
        )

    offsets = far_first(side)

    def dev_d(dd):
        return (pipe, dd, t)

    def dev_t(tt):
        return (pipe, d, tt)

    barrier = pltpu.get_barrier_semaphore()
    for dx, dy in offsets:
        pl.semaphore_signal(barrier, inc=1, device_id=dev_d(at_xy(dx, dy)), device_id_type=MESH)
    for dt in range(1, n_t):
        pl.semaphore_signal(barrier, inc=1, device_id=dev_t(at_z(dt)), device_id_type=MESH)

    @pl.when(pipe < n_pipe - 1)
    def _():
        pl.semaphore_signal(barrier, inc=1, device_id=(pipe + 1, d, t), device_id_type=MESH)

    rows_d = pl.ds(pl.multiple_of(d * blk, blk), blk)
    wcol = pl.multiple_of(t * two, two)
    own_k = local(kw_hbm.at[rows_d], wg_v.at[:, pl.ds(wcol, head)], 0)
    own_v = local(vw_hbm.at[rows_d], wg_v.at[:, pl.ds(wcol + head, head)], 1)
    gain_c = local(gain_hbm, gain_v, 2)

    lo = lax.rem(t, 2)
    hi = t // 2
    partner = t + 1 - 2 * lo
    order_q = (0, 2, 1, 3)

    def rows_of(i):
        return pl.ds(pl.multiple_of(lax.rem(t + i, n_t) * quarter, quarter), quarter)

    x_cs = {i: local(x_hbm.at[rows_of(i)], x_v.at[rows_of(i)], 3 + i) for i in order_q}
    n_w = 4
    wrows = width // n_w
    w_cs = []
    for i in range(n_w):
        r = pl.ds(i * wrows, wrows)
        w_cs.append(local(kw_hbm.at[r], w_v.at[r, pl.ds(0, head)], 7 + 2 * i))
        w_cs.append(local(vw_hbm.at[r], w_v.at[r, pl.ds(head, head)], 8 + 2 * i))
    seg_c = local(seg_hbm, seg_v, 15)
    q_c = local(q_hbm, q_v, 16)
    oc_c = local(oc_hbm, oc_v, 17)
    up_c = local(up_hbm, up_v, 18)

    step = 512

    def norm_quarter(i):
        r = rows_of(i)
        acc = jnp.zeros((quarter, 128), F32)
        for c in range(0, width, step):
            xf = x_v[r, c:c + step].astype(F32)
            sq = xf * xf
            for j in range(0, step, 128):
                acc = acc + sq[:, j:j + 128]
        mean = jnp.sum(acc, axis=-1, keepdims=True) * (1.0 / width)
        inv = lax.rsqrt(mean + NORM_EPS)
        for c in range(0, width, step):
            xf = x_v[r, c:c + step].astype(F32)
            normed = (xf * inv * gain_v[:, c:c + step]).astype(BF16)
            qi = lax.rem(t + i, n_t)
            n_v[qi // 2, lax.rem(qi, 2), :, c:c + step] = normed
        return inv

    own_k.wait()
    own_v.wait()
    peers = len(offsets) + n_t - 1

    @pl.when(pipe > 0)
    def _():
        pl.semaphore_wait(barrier, peers + 1)

    @pl.when(pipe == 0)
    def _():
        pl.semaphore_wait(barrier, peers)

    own_rows = rows_of(0)
    w_pieces = 4
    prow = blk // w_pieces

    def w_copy(lane, r, q, src, dev):
        cols = pl.ds(pl.multiple_of(src * two, two), two)
        ref = wg_v.at[pl.ds(q * prow, prow), cols]
        return remote(ref, ref, ws_s, ws_r, (r * w_pieces + q) * 2 + lane, dev_t(dev))

    def w_round(r, pieces):
        for q in pieces:
            @pl.when((t - r >= 0) & (t < n_t - 1))
            def _():
                w_copy(0, r, q, t - r, t + 1).start()

            @pl.when((t + r < n_t) & (t > 0))
            def _():
                w_copy(1, r, q, t + r, t - 1).start()

    def w_arrived(r, q):
        @pl.when(t - r - 1 >= 0)
        def _():
            w_copy(0, r, q, t, t).wait_recv()

        @pl.when(t + r + 1 < n_t)
        def _():
            w_copy(1, r, q, t, t).wait_recv()

    def w_sent(r, q):
        @pl.when((t - r >= 0) & (t < n_t - 1))
        def _():
            w_copy(0, r, q, t, t).wait_send()

        @pl.when((t + r < n_t) & (t > 0))
        def _():
            w_copy(1, r, q, t, t).wait_send()

    def w_forward(r):
        for q in range(w_pieces):
            w_arrived(r - 1, q)

            @pl.when((t - r >= 0) & (t < n_t - 1))
            def _():
                w_copy(0, r, q, t - r, t + 1).start()

            @pl.when((t + r < n_t) & (t > 0))
            def _():
                w_copy(1, r, q, t + r, t - 1).start()

    w_round(0, range(w_pieces // 2))

    gain_c.wait()
    x_cs[0].wait()
    inv_v[...] = jnp.broadcast_to(norm_quarter(0), (quarter, 128))
    x_cs[2].wait()
    norm_quarter(2)

    def blk_cols(dd):
        return pl.ds(pl.multiple_of(dd * blk, blk), blk)

    nw = blk // 2

    def part_cols(dd, p):
        return pl.ds(pl.multiple_of(dd * blk + p * nw, nw), nw)

    oth = 1 - hi
    n_sends = []
    for i, (dx, dy) in enumerate(offsets):
        dd = at_xy(dx, dy)
        c = remote(n_v.at[hi, lo, :, blk_cols(dd)], nx_v.at[my, mx, hi], nx_s, nx_r, i, dev_d(dd))
        c.start()
        n_sends.append(c)
    nx_v[my, mx] = n_v[:, lo, :, blk_cols(d)]

    def others(p):
        for i, (dx, dy) in enumerate(offsets):
            dd = at_xy(dx, dy)
            yield remote(
                n_v.at[oth, lo, :, part_cols(dd, p)], nx_v.at[my, mx, oth, :, pl.ds(p * nw, nw)],
                nx_s, nx_r, (p + 1) * len(offsets) + i, dev_d(dd),
            )

    def send_other(p):
        for c in others(p):
            c.start()

    send_other(0)

    for i in (1, 3):
        x_cs[i].wait()
        norm_quarter(i)

    kv = jnp.zeros((seq, two), F32)
    for i in range(n_w):
        w_cs[2 * i].wait()
        w_cs[2 * i + 1].wait()
        kv = kv + jnp.dot(
            n_v[:, :, :, i * wrows:(i + 1) * wrows].reshape(seq, wrows), w_v[i * wrows:(i + 1) * wrows, :],
            preferred_element_type=F32,
        )
    keys = kv[:, :head].astype(BF16)
    values = kv[:, head:].astype(BF16)

    factor = 1.0 / math.sqrt(head)
    seg_c.wait()
    seg_r = jnp.broadcast_to(seg_v[...], (seq, seq))
    ri = lax.broadcasted_iota(jnp.int32, (seq, seq), 0)
    ci = lax.broadcasted_iota(jnp.int32, (seq, seq), 1)
    allowed1 = (ci <= ri) & (seg_r == seg_r.T)
    allowed = jnp.concatenate([allowed1.astype(F32)] * group, axis=0) > 0.5
    q_c.wait()
    oc_c.wait()
    qs = jnp.concatenate([q_v[:, g * head:(g + 1) * head] for g in range(group)], axis=0)
    ocs = jnp.concatenate([oc_v[:, g * head:(g + 1) * head] for g in range(group)], axis=0)
    nt = (((1,), (1,)), ((), ()))
    tn = (((0,), (0,)), ((), ()))
    s = lax.dot_general(qs, keys, nt, preferred_element_type=F32) * factor
    dprob = lax.dot_general(ocs, values, nt, preferred_element_type=F32)
    e = jnp.where(allowed, jnp.exp(s), 0.0)
    probs = e / jnp.sum(e, axis=-1, keepdims=True)
    inner = jnp.sum(probs * dprob, axis=-1, keepdims=True)
    ds_ = (probs * (dprob - inner)).astype(BF16)
    pb = probs.astype(BF16)
    dk = (lax.dot_general(ds_, qs, tn, preferred_element_type=F32) * factor).astype(BF16)
    dv = lax.dot_general(pb, ocs, tn, preferred_element_type=F32).astype(BF16)
    dkv_v[:, :head] = dk
    dkv_v[:, head:] = dv
    msum = jnp.sum(
        dk.astype(F32) * kv[:, :head] + dv.astype(F32) * kv[:, head:], axis=-1, keepdims=True
    )
    mfull = jnp.broadcast_to(msum, (seq, 128))
    mtop = mfull.astype(BF16)
    mlow = (mfull - mtop.astype(F32)).astype(BF16)
    lane = lax.broadcasted_iota(jnp.int32, (seq, 128), 1)
    mp_v[...] = jnp.where(lane < 64, mtop.astype(F32), mlow.astype(F32)).astype(BF16)

    def head_cols(h):
        return pl.ds(pl.multiple_of(h * two + (h // 2) * 128, 128), two)

    def extra_cols(par):
        return pl.ds(pl.multiple_of(par * two, two), two)

    z_sends = []
    for dt in range(1, n_t):
        tt = at_z(dt)
        r = pl.ds(pl.multiple_of(tt * quarter, quarter), quarter)
        c = remote(dkv_v.at[r], ag_v.at[my, mx, :, head_cols(t)], zk_s, zk_r, dt - 1, dev_t(tt))
        c.start()
        z_sends.append(c)
    r = pl.ds(pl.multiple_of(lax.rem(partner + 2, n_t) * quarter, quarter), quarter)
    c = remote(dkv_v.at[r], ax_v.at[my, mx, :, extra_cols(lo)], zk_s, zk_r, n_t - 1, dev_t(partner))
    c.start()
    z_sends.append(c)
    m_sends = []
    for dt in range(1, n_t):
        tt = at_z(dt)
        r = pl.ds(pl.multiple_of(tt * quarter, quarter), quarter)
        c = remote(mp_v.at[r], mr_v.at[dt], zm_s, zm_r, dt - 1, dev_t(tt))
        c.start()
        m_sends.append(c)
    w_round(0, range(w_pieces // 2, w_pieces))
    ag_v[my, mx, :, head_cols(t)] = dkv_v[own_rows, :]
    ax_v[my, mx, :, extra_cols(lo)] = dkv_v[rows_of(2), :]
    mr_v[0] = mp_v[own_rows, :]

    for c in z_sends:
        c.wait()
    for c in m_sends:
        c.wait()

    m = mr_v[0].astype(F32)
    for h in range(1, n_t):
        m = m + mr_v[h].astype(F32)
    m = (m[:, :1] + m[:, 64:65]) * (1.0 / width)
    lane = lax.broadcasted_iota(jnp.int32, (quarter, 128), 1)
    inv_f = inv_v[...]
    both = jnp.where(lane < 64, inv_f, inv_f * m)
    top = both.astype(BF16).astype(F32)
    fine = lax.rem(lane, 64) >= 32
    ag_v[my, mx, :, 2 * two:2 * two + 128] = jnp.where(fine, both - top, top).astype(BF16)

    order = sorted(range(1, side), key=lambda i: -min(i, side - i))
    na = side - 1

    class Gather:
        def __init__(self, buf, ss, rs, cuts):
            self.buf, self.ss, self.rs, self.cuts = buf, ss, rs, cuts

        def piece(self, h, yy, xx):
            return self.buf.at[yy, xx, :, pl.ds(*self.cuts[h])]

        def copy(self, ref, i, axis, n):
            dd = at_xy(i, 0) if axis == 0 else at_xy(0, i)
            return remote(ref, ref, self.ss, self.rs, n, dev_d(dd))

        def first(self, i, h):
            return self.copy(self.piece(h, my, mx), i, h, h * na + i - 1)

        def second(self, i, h, j):
            yy = my if h == 0 else lax.rem(my + side - i, side)
            xx = mx if h == 1 else lax.rem(mx + side - i, side)
            n = 2 * na + (h * side + i) * na + j - 1
            return self.copy(self.piece(h, yy, xx), j, 1 - h, n)

        def begin(self):
            for i in order:
                for h in range(2):
                    self.first(i, h).start()
            self.spread(0, 0)
            self.spread(0, 1)

        def spread(self, i, h):
            for j in order:
                self.second(i, h, j).start()

        def forward(self):
            for i in order:
                for h in range(2):
                    self.first(i, h).wait_recv()
                    self.spread(i, h)

        def finish(self):
            for i in order:
                for h in range(2):
                    self.first(i, h).wait_send()
            for i in range(side):
                for h in range(2):
                    for j in order:
                        self.second(i, h, j).wait()

    cut = 2 * two + 128
    main = Gather(ag_v, a1_s, a1_r, ((0, cut), (cut, 2 * two)))
    extra = Gather(ax_v, a2_s, a2_r, ((0, two), (two, two)))
    main.begin()
    w_forward(1)

    dq = (jnp.dot(ds_, keys, preferred_element_type=F32) * factor).astype(BF16)
    for g in range(group):
        dq_out[:, g * head:(g + 1) * head] = dq[g * seq:(g + 1) * seq, :]

    main.forward()
    w_forward(2)
    for c in n_sends:
        c.wait()
    main.finish()
    @pl.when(pipe < n_pipe - 2)
    def _():
        extra.begin()
        send_other(1)


    for q in range(w_pieces):
        w_arrived(2, q)
    tokens = n_dp * quarter
    row = side * quarter
    gain_b = gain_v[:, blk_cols(d)]
    gain_r = 1.0 / gain_b
    prev = (lax.rem(pipe + n_pipe - 1, n_pipe), d, t)
    dys = (2, 1, 3, 0)

    def chain_copies(j):
        return [remote(sb_v.at[j], sr_v.at[j], c_s, c_r, j, prev)]

    def chain_send(j):
        for c in chain_copies(j):
            c.start()

    def chain_take(j):
        for c in chain_copies(j):
            c.wait_recv()

    def deliver(j):
        dy = dys[j]
        for dx in range(side):
            i = j * side + dx
            if dx or dy:
                deliver_copy(i).start()
            else:
                fr_v[i] = sb_v[j, mx]

    def deliver_copy(i):
        dx, dy = i % side, dys[i // side]
        src = sb_v.at[i // side, lax.rem(mx + dx, side)]
        return remote(src, fr_v.at[i], g_s, g_r, i, dev_d(at_xy(dx, dy)))

    def chain(j):
        chain_take(j)
        tot = cf_v[j] + sr_v[j].reshape(row, blk).astype(F32)
        sb_v[j] = tot.astype(BF16).reshape(side, quarter, blk)

        @pl.when(pipe > 0)
        def _():
            chain_send(j)

    for j, dy in enumerate(dys):
        yy = lax.rem(my + dy, side)
        lhs = ag_v[yy, :, :, :2 * two].reshape(row, 2 * two)
        g = lax.dot_general(lhs, wg_v[:, :2 * two], nt, preferred_element_type=F32)
        lhs = ag_v[yy, :, :, cut:].reshape(row, 2 * two)
        g = g + lax.dot_general(lhs, wg_v[:, 2 * two:], nt, preferred_element_type=F32)
        sc = ag_v[yy, :, :, 2 * two:cut].reshape(row, 128).astype(F32)
        alpha = sc[:, :1] + sc[:, 32:33]
        beta = sc[:, 64:65] + sc[:, 96:97]
        nrm = nx_v[yy, :, hi].reshape(row, blk).astype(F32)
        con = alpha * (gain_b * g) - (beta * nrm) * gain_r
        cf_v[j] = con

        @pl.when(pipe == n_pipe - 1)
        def _():
            sb_v[j] = con.astype(BF16).reshape(side, quarter, blk)
            chain_send(j)

        if j:
            @pl.when(pipe == n_pipe - 2)
            def _():
                chain(j - 1)

    @pl.when(pipe == n_pipe - 2)
    def _():
        chain(side - 1)

    @pl.when(pipe >= n_pipe - 2)
    def _():
        for j in range(side):
            deliver(j)

    @pl.when(pipe >= n_pipe - 2)
    def _():
        extra.begin()
        send_other(1)

    extra.forward()

    for p in range(2):
        for c in others(p):
            c.wait()
    extra.finish()
    nxt_own = nx_v[:, :, hi].reshape(tokens, blk).T
    nxt_oth = nx_v[:, :, oth].reshape(tokens, blk).T
    pair_at = pl.multiple_of(hi * (2 * two + 128), 128)
    own_pair = ag_v[:, :, :, pl.ds(pair_at, 2 * two)]
    part = jnp.dot(nxt_own, own_pair.reshape(tokens, 2 * two), preferred_element_type=F32)
    part = part + jnp.dot(
        nxt_oth, ax_v[...].reshape(tokens, 2 * two), preferred_element_type=F32
    )
    for h in range(2):
        pw_v[h] = part[:, h * two:(h + 1) * two]
    ps_v[...] = pw_v[1 - lo].astype(BF16)
    p_c = remote(ps_v, pr_v, p_s, p_r, 0, dev_t(partner))
    p_c.start()

    @pl.when(pipe < n_pipe - 2)
    def _():
        for j in range(side):
            chain(j)
            deliver(j)

    up_c.wait()
    for i in range(n_dp):
        dx, dy = i % side, dys[i // side]
        if dx or dy:
            deliver_copy(i).wait_recv()
        cc = blk_cols(at_xy(side - dx, side - dy))
        sc_out[:, cc] = (up_v[:, cc].astype(F32) + fr_v[i].astype(F32)).astype(BF16)

    p_c.wait()
    tot = pw_v[lo] + pr_v[...].astype(F32)
    kg_out[...] = tot[:, :head]
    vg_out[...] = tot[:, head:]
    for i in range(n_dp):
        if i % side or dys[i // side]:
            deliver_copy(i).wait_send()
    for r in range(n_t - 1):
        for q in range(w_pieces):
            w_sent(r, q)

    @pl.when(pipe > 0)
    def _():
        for j in range(side):
            for c in chain_copies(j):
                c.wait_send()


def write_out(*refs):
    n = 4
    ins, outs, sems = refs[:n], refs[n:2 * n], refs[2 * n]
    stores = [pltpu.make_async_copy(ins[i], outs[i], sems.at[i]) for i in range(n)]
    for o in stores:
        o.start()
    for o in stores:
        o.wait()


def per_device(sizes, section_input, norm_gain, key_weight, value_weight, queries, out_cotangent,
               segment_ids, upstream):
    n_pipe, n_dp, n_t = sizes
    seq, width = section_input.shape[3:]
    head = key_weight.shape[2]
    group = queries.shape[4] // head
    side = math.isqrt(n_dp)
    blk = width // n_dp
    quarter = seq // n_t
    two = 2 * head
    heads = group * head
    dims = (n_pipe, n_dp, n_t, side, seq, width, head, group)
    V = pltpu.VMEM
    DMA = pltpu.SemaphoreType.DMA
    any_spec = pl.BlockSpec(memory_space=pl.ANY)
    noff = n_dp - 1
    nz = n_t - 1
    na = 2 * (side - 1)
    sc, dq, kg, vg = pl.pallas_call(
        functools.partial(kernel, dims),
        out_shape=(
            V((quarter, width), BF16),
            V((seq, heads), BF16),
            V((blk, head), F32),
            V((blk, head), F32),
        ),
        in_specs=[any_spec] * 8,
        out_specs=(pl.BlockSpec(memory_space=V),) * 4,
        scratch_shapes=[
            V((seq, width), BF16),
            V((2, 2, quarter, width), BF16),
            V((width, two), BF16),
            V((blk, n_t * two), BF16),
            V((seq, heads), BF16),
            V((seq, heads), BF16),
            V((1, seq), jnp.int32),
            V((quarter, width), BF16),
            V((1, width), F32),
            V((quarter, 128), F32),
            V((side, side, 2, quarter, blk), BF16),
            V((seq, two), BF16),
            V((seq, 128), BF16),
            V((n_t, quarter, 128), BF16),
            V((side, side, quarter, n_t * two + 128), BF16),
            V((side, side, quarter, 2 * two), BF16),
            V((side, side * quarter, blk), F32),
            V((n_dp, quarter, blk), BF16),
            V((side, side, quarter, blk), BF16),
            V((side, side, quarter, blk), BF16),
            V((2, blk, two), F32),
            V((blk, two), BF16),
            V((blk, two), BF16),
            DMA((19,)),
            DMA((8 * nz,)), DMA((8 * nz,)),
            DMA((3 * noff,)), DMA((3 * noff,)),
            DMA((n_t,)), DMA((n_t,)),
            DMA((nz,)), DMA((nz,)),
            DMA((na + side * na,)), DMA((na + side * na,)),
            DMA((na + side * na,)), DMA((na + side * na,)),
            DMA((n_dp,)), DMA((n_dp,)),
            DMA((n_dp,)), DMA((n_dp,)),
            DMA((1,)), DMA((1,)),
        ],
        compiler_params=pltpu.CompilerParams(
            collective_id=0, has_side_effects=True, vmem_limit_bytes=62 << 20
        ),
        name="attention_backward",
    )(
        section_input.reshape(seq, width),
        norm_gain.reshape(1, width),
        key_weight.reshape(width, head),
        value_weight.reshape(width, head),
        queries.reshape(seq, heads),
        out_cotangent.reshape(seq, heads),
        segment_ids.reshape(1, seq),
        upstream.reshape(quarter, width),
    )
    parts = (sc, dq, kg, vg)
    sc, dq, kg, vg = pl.pallas_call(
        write_out,
        out_shape=tuple(jax.ShapeDtypeStruct(a.shape, a.dtype) for a in parts),
        in_specs=[pl.BlockSpec(memory_space=V)] * 4,
        out_specs=(any_spec,) * 4,
        scratch_shapes=[DMA((4,))],
        compiler_params=pltpu.CompilerParams(vmem_limit_bytes=16 << 20),
        name="write_out",
    )(*parts)
    return (
        sc.reshape(1, 1, 1, quarter, width),
        dq.reshape(1, 1, 1, seq, heads),
        kg[None],
        vg[None],
    )


def solution(mesh):
    sizes = tuple(mesh.shape[a] for a in ("pipe", "dp", "tensor"))
    return jax.shard_map(
        functools.partial(per_device, sizes),
        mesh=mesh,
        in_specs=(
            P("pipe", None, "dp", None, None),
            P("pipe", None),
            P("pipe", None, "tensor"),
            P("pipe", None, "tensor"),
            P("pipe", None, "dp", None, "tensor"),
            P("pipe", None, "dp", None, "tensor"),
            P(None, "dp", None),
            P(None, "dp", "tensor", None),
        ),
        out_specs=(
            P("pipe", None, "dp", "tensor", None),
            P("pipe", None, "dp", None, "tensor"),
            P("pipe", "dp", "tensor"),
            P("pipe", "dp", "tensor"),
        ),
        check_vma=False,
    )
```

```python
import functools
import math

import jax
import jax.numpy as jnp
from jax import lax
from jax.experimental import pallas as pl
from jax.experimental.pallas import tpu as pltpu
from jax.sharding import PartitionSpec as P

NORM_EPS = 1e-05
MESH = pl.DeviceIdType.MESH
F32 = jnp.float32
BF16 = jnp.bfloat16


def far_first(side):
    def hops(o):
        return sum(min(a, side - a) for a in o)

    every = [(dx, dy) for dy in range(side) for dx in range(side) if dx or dy]
    return sorted(every, key=hops, reverse=True)


def kernel(
    dims,
    x_hbm, gain_hbm, kw_hbm, vw_hbm, q_hbm, oc_hbm, seg_hbm, up_hbm,
    sc_out, dq_out, kg_out, vg_out,
    x_v, n_v, w_v, wg_v, q_v, oc_v, seg_v, up_v, gain_v, inv_v,
    nx_v, dkv_v, mp_v, mr_v, ag_v, ax_v, cf_v, fr_v, sr_v, sb_v,
    pw_v, ps_v, pr_v,
    ld, ws_s, ws_r, nx_s, nx_r, zk_s, zk_r, zm_s, zm_r,
    a1_s, a1_r, a2_s, a2_r, g_s, g_r, c_s, c_r, p_s, p_r,
):
    n_pipe, n_dp, n_t, side, seq, width, head, group = dims
    blk = width // n_dp
    quarter = seq // n_t
    two = 2 * head
    pipe = lax.axis_index("pipe")
    d = lax.axis_index("dp")
    t = lax.axis_index("tensor")
    mx = lax.rem(d, side)
    my = d // side

    def at_xy(dx, dy):
        return lax.rem(my + dy, side) * side + lax.rem(mx + dx, side)

    def at_z(dt):
        return lax.rem(t + dt, n_t)

    def local(src, dst, i):
        c = pltpu.make_async_copy(src, dst, ld.at[i])
        c.start()
        return c

    def remote(src, dst, ss, rs, i, dev):
        return pltpu.make_async_remote_copy(
            src_ref=src, dst_ref=dst, send_sem=ss.at[i], recv_sem=rs.at[i],
            device_id=dev, device_id_type=MESH,
        )

    offsets = far_first(side)

    def dev_d(dd):
        return (pipe, dd, t)

    def dev_t(tt):
        return (pipe, d, tt)

    barrier = pltpu.get_barrier_semaphore()
    for dx, dy in offsets:
        pl.semaphore_signal(barrier, inc=1, device_id=dev_d(at_xy(dx, dy)), device_id_type=MESH)
    for dt in range(1, n_t):
        pl.semaphore_signal(barrier, inc=1, device_id=dev_t(at_z(dt)), device_id_type=MESH)

    @pl.when(pipe < n_pipe - 1)
    def _():
        pl.semaphore_signal(barrier, inc=1, device_id=(pipe + 1, d, t), device_id_type=MESH)

    rows_d = pl.ds(pl.multiple_of(d * blk, blk), blk)
    wcol = pl.multiple_of(t * two, two)
    own_k = local(kw_hbm.at[rows_d], wg_v.at[:, pl.ds(wcol, head)], 0)
    own_v = local(vw_hbm.at[rows_d], wg_v.at[:, pl.ds(wcol + head, head)], 1)
    gain_c = local(gain_hbm, gain_v, 2)

    lo = lax.rem(t, 2)
    hi = t // 2
    partner = t + 1 - 2 * lo
    order_q = (0, 2, 1, 3)

    def rows_of(i):
        return pl.ds(pl.multiple_of(lax.rem(t + i, n_t) * quarter, quarter), quarter)

    x_cs = {i: local(x_hbm.at[rows_of(i)], x_v.at[rows_of(i)], 3 + i) for i in order_q}
    n_w = 4
    wrows = width // n_w
    w_cs = []
    for i in range(n_w):
        r = pl.ds(i * wrows, wrows)
        w_cs.append(local(kw_hbm.at[r], w_v.at[r, pl.ds(0, head)], 7 + 2 * i))
        w_cs.append(local(vw_hbm.at[r], w_v.at[r, pl.ds(head, head)], 8 + 2 * i))
    seg_c = local(seg_hbm, seg_v, 15)
    q_c = local(q_hbm, q_v, 16)
    oc_c = local(oc_hbm, oc_v, 17)
    up_c = local(up_hbm, up_v, 18)

    step = 512

    def norm_quarter(i):
        r = rows_of(i)
        acc = jnp.zeros((quarter, 128), F32)
        for c in range(0, width, step):
            xf = x_v[r, c:c + step].astype(F32)
            sq = xf * xf
            for j in range(0, step, 128):
                acc = acc + sq[:, j:j + 128]
        mean = jnp.sum(acc, axis=-1, keepdims=True) * (1.0 / width)
        inv = lax.rsqrt(mean + NORM_EPS)
        for c in range(0, width, step):
            xf = x_v[r, c:c + step].astype(F32)
            normed = (xf * inv * gain_v[:, c:c + step]).astype(BF16)
            qi = lax.rem(t + i, n_t)
            n_v[qi // 2, lax.rem(qi, 2), :, c:c + step] = normed
        return inv

    own_k.wait()
    own_v.wait()
    peers = len(offsets) + n_t - 1

    @pl.when(pipe > 0)
    def _():
        pl.semaphore_wait(barrier, peers + 1)

    @pl.when(pipe == 0)
    def _():
        pl.semaphore_wait(barrier, peers)

    own_rows = rows_of(0)
    w_pieces = 2
    prow = blk // w_pieces

    def w_copy(lane, r, q, src, dev):
        cols = pl.ds(pl.multiple_of(src * two, two), two)
        ref = wg_v.at[pl.ds(q * prow, prow), cols]
        return remote(ref, ref, ws_s, ws_r, (r * w_pieces + q) * 2 + lane, dev_t(dev))

    def w_round(r, pieces):
        for q in pieces:
            @pl.when((t - r >= 0) & (t < n_t - 1))
            def _():
                w_copy(0, r, q, t - r, t + 1).start()

            @pl.when((t + r < n_t) & (t > 0))
            def _():
                w_copy(1, r, q, t + r, t - 1).start()

    def w_arrived(r, q):
        @pl.when(t - r - 1 >= 0)
        def _():
            w_copy(0, r, q, t, t).wait_recv()

        @pl.when(t + r + 1 < n_t)
        def _():
            w_copy(1, r, q, t, t).wait_recv()

    def w_sent(r, q):
        @pl.when((t - r >= 0) & (t < n_t - 1))
        def _():
            w_copy(0, r, q, t, t).wait_send()

        @pl.when((t + r < n_t) & (t > 0))
        def _():
            w_copy(1, r, q, t, t).wait_send()

    def w_forward(r):
        for q in range(w_pieces):
            w_arrived(r - 1, q)

            @pl.when((t - r >= 0) & (t < n_t - 1))
            def _():
                w_copy(0, r, q, t - r, t + 1).start()

            @pl.when((t + r < n_t) & (t > 0))
            def _():
                w_copy(1, r, q, t + r, t - 1).start()

    w_round(0, range(w_pieces // 2))

    gain_c.wait()
    x_cs[0].wait()
    inv_v[...] = jnp.broadcast_to(norm_quarter(0), (quarter, 128))
    x_cs[2].wait()
    norm_quarter(2)

    def blk_cols(dd):
        return pl.ds(pl.multiple_of(dd * blk, blk), blk)

    nw = blk // 2

    def part_cols(dd, p):
        return pl.ds(pl.multiple_of(dd * blk + p * nw, nw), nw)

    oth = 1 - hi
    n_sends = []
    for i, (dx, dy) in enumerate(offsets):
        dd = at_xy(dx, dy)
        c = remote(n_v.at[hi, lo, :, blk_cols(dd)], nx_v.at[my, mx, hi], nx_s, nx_r, i, dev_d(dd))
        c.start()
        n_sends.append(c)
    nx_v[my, mx] = n_v[:, lo, :, blk_cols(d)]

    def others(p):
        for i, (dx, dy) in enumerate(offsets):
            dd = at_xy(dx, dy)
            yield remote(
                n_v.at[oth, lo, :, part_cols(dd, p)], nx_v.at[my, mx, oth, :, pl.ds(p * nw, nw)],
                nx_s, nx_r, (p + 1) * len(offsets) + i, dev_d(dd),
            )

    def send_other(p):
        for c in others(p):
            c.start()

    send_other(0)

    for i in (1, 3):
        x_cs[i].wait()
        norm_quarter(i)

    kv = jnp.zeros((seq, two), F32)
    for i in range(n_w):
        w_cs[2 * i].wait()
        w_cs[2 * i + 1].wait()
        kv = kv + jnp.dot(
            n_v[:, :, :, i * wrows:(i + 1) * wrows].reshape(seq, wrows), w_v[i * wrows:(i + 1) * wrows, :],
            preferred_element_type=F32,
        )
    keys = kv[:, :head].astype(BF16)
    values = kv[:, head:].astype(BF16)

    factor = 1.0 / math.sqrt(head)
    seg_c.wait()
    seg_r = jnp.broadcast_to(seg_v[...], (seq, seq))
    ri = lax.broadcasted_iota(jnp.int32, (seq, seq), 0)
    ci = lax.broadcasted_iota(jnp.int32, (seq, seq), 1)
    allowed1 = (ci <= ri) & (seg_r == seg_r.T)
    allowed = jnp.concatenate([allowed1.astype(F32)] * group, axis=0) > 0.5
    q_c.wait()
    oc_c.wait()
    qs = jnp.concatenate([q_v[:, g * head:(g + 1) * head] for g in range(group)], axis=0)
    ocs = jnp.concatenate([oc_v[:, g * head:(g + 1) * head] for g in range(group)], axis=0)
    nt = (((1,), (1,)), ((), ()))
    tn = (((0,), (0,)), ((), ()))
    s = lax.dot_general(qs, keys, nt, preferred_element_type=F32) * factor
    dprob = lax.dot_general(ocs, values, nt, preferred_element_type=F32)
    e = jnp.where(allowed, jnp.exp(s), 0.0)
    probs = e / jnp.sum(e, axis=-1, keepdims=True)
    inner = jnp.sum(probs * dprob, axis=-1, keepdims=True)
    ds_ = (probs * (dprob - inner)).astype(BF16)
    pb = probs.astype(BF16)
    dk = (lax.dot_general(ds_, qs, tn, preferred_element_type=F32) * factor).astype(BF16)
    dv = lax.dot_general(pb, ocs, tn, preferred_element_type=F32).astype(BF16)
    dkv_v[:, :head] = dk
    dkv_v[:, head:] = dv
    msum = jnp.sum(
        dk.astype(F32) * kv[:, :head] + dv.astype(F32) * kv[:, head:], axis=-1, keepdims=True
    )
    mfull = jnp.broadcast_to(msum, (seq, 128))
    mtop = mfull.astype(BF16)
    mlow = (mfull - mtop.astype(F32)).astype(BF16)
    lane = lax.broadcasted_iota(jnp.int32, (seq, 128), 1)
    mp_v[...] = jnp.where(lane < 64, mtop.astype(F32), mlow.astype(F32)).astype(BF16)

    def head_cols(h):
        return pl.ds(pl.multiple_of(h * two + (h // 2) * 128, 128), two)

    def extra_cols(par):
        return pl.ds(pl.multiple_of(par * two, two), two)

    z_sends = []
    for dt in range(1, n_t):
        tt = at_z(dt)
        r = pl.ds(pl.multiple_of(tt * quarter, quarter), quarter)
        c = remote(dkv_v.at[r], ag_v.at[my, mx, :, head_cols(t)], zk_s, zk_r, dt - 1, dev_t(tt))
        c.start()
        z_sends.append(c)
    r = pl.ds(pl.multiple_of(lax.rem(partner + 2, n_t) * quarter, quarter), quarter)
    c = remote(dkv_v.at[r], ax_v.at[my, mx, :, extra_cols(lo)], zk_s, zk_r, n_t - 1, dev_t(partner))
    c.start()
    z_sends.append(c)
    m_sends = []
    for dt in range(1, n_t):
        tt = at_z(dt)
        r = pl.ds(pl.multiple_of(tt * quarter, quarter), quarter)
        c = remote(mp_v.at[r], mr_v.at[dt], zm_s, zm_r, dt - 1, dev_t(tt))
        c.start()
        m_sends.append(c)
    w_round(0, range(w_pieces // 2, w_pieces))
    ag_v[my, mx, :, head_cols(t)] = dkv_v[own_rows, :]
    ax_v[my, mx, :, extra_cols(lo)] = dkv_v[rows_of(2), :]
    mr_v[0] = mp_v[own_rows, :]

    for c in z_sends:
        c.wait()
    for c in m_sends:
        c.wait()

    m = mr_v[0].astype(F32)
    for h in range(1, n_t):
        m = m + mr_v[h].astype(F32)
    m = (m[:, :1] + m[:, 64:65]) * (1.0 / width)
    lane = lax.broadcasted_iota(jnp.int32, (quarter, 128), 1)
    inv_f = inv_v[...]
    both = jnp.where(lane < 64, inv_f, inv_f * m)
    top = both.astype(BF16).astype(F32)
    fine = lax.rem(lane, 64) >= 32
    ag_v[my, mx, :, 2 * two:2 * two + 128] = jnp.where(fine, both - top, top).astype(BF16)

    order = sorted(range(1, side), key=lambda i: -min(i, side - i))
    na = side - 1

    class Gather:
        def __init__(self, buf, ss, rs, cuts):
            self.buf, self.ss, self.rs, self.cuts = buf, ss, rs, cuts

        def piece(self, h, yy, xx):
            return self.buf.at[yy, xx, :, pl.ds(*self.cuts[h])]

        def copy(self, ref, i, axis, n):
            dd = at_xy(i, 0) if axis == 0 else at_xy(0, i)
            return remote(ref, ref, self.ss, self.rs, n, dev_d(dd))

        def first(self, i, h):
            return self.copy(self.piece(h, my, mx), i, h, h * na + i - 1)

        def second(self, i, h, j):
            yy = my if h == 0 else lax.rem(my + side - i, side)
            xx = mx if h == 1 else lax.rem(mx + side - i, side)
            n = 2 * na + (h * side + i) * na + j - 1
            return self.copy(self.piece(h, yy, xx), j, 1 - h, n)

        def begin(self):
            for i in order:
                for h in range(2):
                    self.first(i, h).start()
            self.spread(0, 0)
            self.spread(0, 1)

        def spread(self, i, h):
            for j in order:
                self.second(i, h, j).start()

        def forward(self):
            for i in order:
                for h in range(2):
                    self.first(i, h).wait_recv()
                    self.spread(i, h)

        def finish(self):
            for i in order:
                for h in range(2):
                    self.first(i, h).wait_send()
            for i in range(side):
                for h in range(2):
                    for j in order:
                        self.second(i, h, j).wait()

    cut = 2 * two + 128
    main = Gather(ag_v, a1_s, a1_r, ((0, cut), (cut, 2 * two)))
    extra = Gather(ax_v, a2_s, a2_r, ((0, two), (two, two)))
    main.begin()
    w_forward(1)

    dq = (jnp.dot(ds_, keys, preferred_element_type=F32) * factor).astype(BF16)
    for g in range(group):
        dq_out[:, g * head:(g + 1) * head] = dq[g * seq:(g + 1) * seq, :]

    main.forward()
    w_forward(2)
    for c in n_sends:
        c.wait()
    main.finish()
    @pl.when(pipe < n_pipe - 2)
    def _():
        extra.begin()
        send_other(1)


    for q in range(w_pieces):
        w_arrived(2, q)
    tokens = n_dp * quarter
    row = side * quarter
    gain_b = gain_v[:, blk_cols(d)]
    gain_r = 1.0 / gain_b
    prev = (lax.rem(pipe + n_pipe - 1, n_pipe), d, t)
    dys = (2, 1, 3, 0)

    def chain_copies(j):
        return [remote(sb_v.at[j], sr_v.at[j], c_s, c_r, j, prev)]

    def chain_send(j):
        for c in chain_copies(j):
            c.start()

    def chain_take(j):
        for c in chain_copies(j):
            c.wait_recv()

    def deliver(j):
        dy = dys[j]
        for dx in range(side):
            i = j * side + dx
            if dx or dy:
                deliver_copy(i).start()
            else:
                fr_v[i] = sb_v[j, mx]

    def deliver_copy(i):
        dx, dy = i % side, dys[i // side]
        src = sb_v.at[i // side, lax.rem(mx + dx, side)]
        return remote(src, fr_v.at[i], g_s, g_r, i, dev_d(at_xy(dx, dy)))

    def chain(j):
        chain_take(j)
        tot = cf_v[j] + sr_v[j].reshape(row, blk).astype(F32)
        sb_v[j] = tot.astype(BF16).reshape(side, quarter, blk)

        @pl.when(pipe > 0)
        def _():
            chain_send(j)

    for j, dy in enumerate(dys):
        yy = lax.rem(my + dy, side)
        lhs = ag_v[yy, :, :, :2 * two].reshape(row, 2 * two)
        g = lax.dot_general(lhs, wg_v[:, :2 * two], nt, preferred_element_type=F32)
        lhs = ag_v[yy, :, :, cut:].reshape(row, 2 * two)
        g = g + lax.dot_general(lhs, wg_v[:, 2 * two:], nt, preferred_element_type=F32)
        sc = ag_v[yy, :, :, 2 * two:cut].reshape(row, 128).astype(F32)
        alpha = sc[:, :1] + sc[:, 32:33]
        beta = sc[:, 64:65] + sc[:, 96:97]
        nrm = nx_v[yy, :, hi].reshape(row, blk).astype(F32)
        con = alpha * (gain_b * g) - (beta * nrm) * gain_r
        cf_v[j] = con

        @pl.when(pipe == n_pipe - 1)
        def _():
            sb_v[j] = con.astype(BF16).reshape(side, quarter, blk)
            chain_send(j)

        if j:
            @pl.when(pipe == n_pipe - 2)
            def _():
                chain(j - 1)

    @pl.when(pipe == n_pipe - 2)
    def _():
        chain(side - 1)

    @pl.when(pipe >= n_pipe - 2)
    def _():
        for j in range(side):
            deliver(j)

    @pl.when(pipe >= n_pipe - 2)
    def _():
        extra.begin()
        send_other(1)

    extra.forward()

    for p in range(2):
        for c in others(p):
            c.wait()
    extra.finish()
    nxt_own = nx_v[:, :, hi].reshape(tokens, blk).T
    nxt_oth = nx_v[:, :, oth].reshape(tokens, blk).T
    pair_at = pl.multiple_of(hi * (2 * two + 128), 128)
    own_pair = ag_v[:, :, :, pl.ds(pair_at, 2 * two)]
    part = jnp.dot(nxt_own, own_pair.reshape(tokens, 2 * two), preferred_element_type=F32)
    part = part + jnp.dot(
        nxt_oth, ax_v[...].reshape(tokens, 2 * two), preferred_element_type=F32
    )
    for h in range(2):
        pw_v[h] = part[:, h * two:(h + 1) * two]
    ps_v[...] = pw_v[1 - lo].astype(BF16)
    p_c = remote(ps_v, pr_v, p_s, p_r, 0, dev_t(partner))
    p_c.start()

    @pl.when(pipe < n_pipe - 2)
    def _():
        for j in range(side):
            chain(j)
            deliver(j)

    up_c.wait()
    for i in range(n_dp):
        dx, dy = i % side, dys[i // side]
        if dx or dy:
            deliver_copy(i).wait_recv()
        cc = blk_cols(at_xy(side - dx, side - dy))
        sc_out[:, cc] = (up_v[:, cc].astype(F32) + fr_v[i].astype(F32)).astype(BF16)

    p_c.wait()
    tot = pw_v[lo] + pr_v[...].astype(F32)
    kg_out[...] = tot[:, :head]
    vg_out[...] = tot[:, head:]
    for i in range(n_dp):
        if i % side or dys[i // side]:
            deliver_copy(i).wait_send()
    for r in range(n_t - 1):
        for q in range(w_pieces):
            w_sent(r, q)

    @pl.when(pipe > 0)
    def _():
        for j in range(side):
            for c in chain_copies(j):
                c.wait_send()


def write_out(*refs):
    n = 4
    ins, outs, sems = refs[:n], refs[n:2 * n], refs[2 * n]
    stores = [pltpu.make_async_copy(ins[i], outs[i], sems.at[i]) for i in range(n)]
    for o in stores:
        o.start()
    for o in stores:
        o.wait()


def per_device(sizes, section_input, norm_gain, key_weight, value_weight, queries, out_cotangent,
               segment_ids, upstream):
    n_pipe, n_dp, n_t = sizes
    seq, width = section_input.shape[3:]
    head = key_weight.shape[2]
    group = queries.shape[4] // head
    side = math.isqrt(n_dp)
    blk = width // n_dp
    quarter = seq // n_t
    two = 2 * head
    heads = group * head
    dims = (n_pipe, n_dp, n_t, side, seq, width, head, group)
    V = pltpu.VMEM
    DMA = pltpu.SemaphoreType.DMA
    any_spec = pl.BlockSpec(memory_space=pl.ANY)
    noff = n_dp - 1
    nz = n_t - 1
    na = 2 * (side - 1)
    sc, dq, kg, vg = pl.pallas_call(
        functools.partial(kernel, dims),
        out_shape=(
            V((quarter, width), BF16),
            V((seq, heads), BF16),
            V((blk, head), F32),
            V((blk, head), F32),
        ),
        in_specs=[any_spec] * 8,
        out_specs=(pl.BlockSpec(memory_space=V),) * 4,
        scratch_shapes=[
            V((seq, width), BF16),
            V((2, 2, quarter, width), BF16),
            V((width, two), BF16),
            V((blk, n_t * two), BF16),
            V((seq, heads), BF16),
            V((seq, heads), BF16),
            V((1, seq), jnp.int32),
            V((quarter, width), BF16),
            V((1, width), F32),
            V((quarter, 128), F32),
            V((side, side, 2, quarter, blk), BF16),
            V((seq, two), BF16),
            V((seq, 128), BF16),
            V((n_t, quarter, 128), BF16),
            V((side, side, quarter, n_t * two + 128), BF16),
            V((side, side, quarter, 2 * two), BF16),
            V((side, side * quarter, blk), F32),
            V((n_dp, quarter, blk), BF16),
            V((side, side, quarter, blk), BF16),
            V((side, side, quarter, blk), BF16),
            V((2, blk, two), F32),
            V((blk, two), BF16),
            V((blk, two), BF16),
            DMA((19,)),
            DMA((8 * nz,)), DMA((8 * nz,)),
            DMA((3 * noff,)), DMA((3 * noff,)),
            DMA((n_t,)), DMA((n_t,)),
            DMA((nz,)), DMA((nz,)),
            DMA((na + side * na,)), DMA((na + side * na,)),
            DMA((na + side * na,)), DMA((na + side * na,)),
            DMA((n_dp,)), DMA((n_dp,)),
            DMA((n_dp,)), DMA((n_dp,)),
            DMA((1,)), DMA((1,)),
        ],
        compiler_params=pltpu.CompilerParams(
            collective_id=0, has_side_effects=True, vmem_limit_bytes=62 << 20
        ),
        name="attention_backward",
    )(
        section_input.reshape(seq, width),
        norm_gain.reshape(1, width),
        key_weight.reshape(width, head),
        value_weight.reshape(width, head),
        queries.reshape(seq, heads),
        out_cotangent.reshape(seq, heads),
        segment_ids.reshape(1, seq),
        upstream.reshape(quarter, width),
    )
    parts = (sc, dq, kg, vg)
    sc, dq, kg, vg = pl.pallas_call(
        write_out,
        out_shape=tuple(jax.ShapeDtypeStruct(a.shape, a.dtype) for a in parts),
        in_specs=[pl.BlockSpec(memory_space=V)] * 4,
        out_specs=(any_spec,) * 4,
        scratch_shapes=[DMA((4,))],
        compiler_params=pltpu.CompilerParams(vmem_limit_bytes=16 << 20),
        name="write_out",
    )(*parts)
    return (
        sc.reshape(1, 1, 1, quarter, width),
        dq.reshape(1, 1, 1, seq, heads),
        kg[None],
        vg[None],
    )


def solution(mesh):
    sizes = tuple(mesh.shape[a] for a in ("pipe", "dp", "tensor"))
    return jax.shard_map(
        functools.partial(per_device, sizes),
        mesh=mesh,
        in_specs=(
            P("pipe", None, "dp", None, None),
            P("pipe", None),
            P("pipe", None, "tensor"),
            P("pipe", None, "tensor"),
            P("pipe", None, "dp", None, "tensor"),
            P("pipe", None, "dp", None, "tensor"),
            P(None, "dp", None),
            P(None, "dp", "tensor", None),
        ),
        out_specs=(
            P("pipe", None, "dp", "tensor", None),
            P("pipe", None, "dp", None, "tensor"),
            P("pipe", "dp", "tensor"),
            P("pipe", "dp", "tensor"),
        ),
        check_vma=False,
    )
```

```python
import functools
import math

import jax
import jax.numpy as jnp
from jax import lax
from jax.experimental import pallas as pl
from jax.experimental.pallas import tpu as pltpu
from jax.sharding import PartitionSpec as P

NORM_EPS = 1e-05
MESH = pl.DeviceIdType.MESH
F32 = jnp.float32
BF16 = jnp.bfloat16


def far_first(side):
    def hops(o):
        return sum(min(a, side - a) for a in o)

    every = [(dx, dy) for dy in range(side) for dx in range(side) if dx or dy]
    return sorted(every, key=hops, reverse=True)


def kernel(
    dims,
    x_hbm, gain_hbm, kw_hbm, vw_hbm, q_hbm, oc_hbm, seg_hbm, up_hbm,
    sc_out, dq_out, kg_out, vg_out,
    x_v, n_v, w_v, wg_v, q_v, oc_v, seg_v, up_v, gain_v, inv_v,
    nx_v, dkv_v, mp_v, mr_v, ag_v, ax_v, cf_v, fr_v, sr_v, sb_v,
    pw_v, ps_v, pr_v,
    ld, ws_s, ws_r, nx_s, nx_r, zk_s, zk_r, zm_s, zm_r,
    a1_s, a1_r, a2_s, a2_r, g_s, g_r, c_s, c_r, p_s, p_r,
):
    n_pipe, n_dp, n_t, side, seq, width, head, group = dims
    blk = width // n_dp
    quarter = seq // n_t
    two = 2 * head
    pipe = lax.axis_index("pipe")
    d = lax.axis_index("dp")
    t = lax.axis_index("tensor")
    mx = lax.rem(d, side)
    my = d // side

    def at_xy(dx, dy):
        return lax.rem(my + dy, side) * side + lax.rem(mx + dx, side)

    def at_z(dt):
        return lax.rem(t + dt, n_t)

    def local(src, dst, i):
        c = pltpu.make_async_copy(src, dst, ld.at[i])
        c.start()
        return c

    def remote(src, dst, ss, rs, i, dev):
        return pltpu.make_async_remote_copy(
            src_ref=src, dst_ref=dst, send_sem=ss.at[i], recv_sem=rs.at[i],
            device_id=dev, device_id_type=MESH,
        )

    offsets = far_first(side)

    def dev_d(dd):
        return (pipe, dd, t)

    def dev_t(tt):
        return (pipe, d, tt)

    barrier = pltpu.get_barrier_semaphore()
    for dx, dy in offsets:
        pl.semaphore_signal(barrier, inc=1, device_id=dev_d(at_xy(dx, dy)), device_id_type=MESH)
    for dt in range(1, n_t):
        pl.semaphore_signal(barrier, inc=1, device_id=dev_t(at_z(dt)), device_id_type=MESH)

    @pl.when(pipe < n_pipe - 1)
    def _():
        pl.semaphore_signal(barrier, inc=1, device_id=(pipe + 1, d, t), device_id_type=MESH)

    rows_d = pl.ds(pl.multiple_of(d * blk, blk), blk)
    wcol = pl.multiple_of(t * two, two)
    own_k = local(kw_hbm.at[rows_d], wg_v.at[:, pl.ds(wcol, head)], 0)
    own_v = local(vw_hbm.at[rows_d], wg_v.at[:, pl.ds(wcol + head, head)], 1)
    gain_c = local(gain_hbm, gain_v, 2)

    lo = lax.rem(t, 2)
    hi = t // 2
    partner = t + 1 - 2 * lo
    order_q = (0, 2, 1, 3)

    def rows_of(i):
        return pl.ds(pl.multiple_of(lax.rem(t + i, n_t) * quarter, quarter), quarter)

    x_cs = {i: local(x_hbm.at[rows_of(i)], x_v.at[rows_of(i)], 3 + i) for i in order_q}
    n_w = 4
    wrows = width // n_w
    w_cs = []
    for i in range(n_w):
        r = pl.ds(i * wrows, wrows)
        w_cs.append(local(kw_hbm.at[r], w_v.at[r, pl.ds(0, head)], 7 + 2 * i))
        w_cs.append(local(vw_hbm.at[r], w_v.at[r, pl.ds(head, head)], 8 + 2 * i))
    seg_c = local(seg_hbm, seg_v, 15)
    q_c = local(q_hbm, q_v, 16)
    oc_c = local(oc_hbm, oc_v, 17)
    up_c = local(up_hbm, up_v, 18)

    step = 512

    def norm_quarter(i):
        r = rows_of(i)
        acc = jnp.zeros((quarter, 128), F32)
        for c in range(0, width, step):
            xf = x_v[r, c:c + step].astype(F32)
            sq = xf * xf
            for j in range(0, step, 128):
                acc = acc + sq[:, j:j + 128]
        mean = jnp.sum(acc, axis=-1, keepdims=True) * (1.0 / width)
        inv = lax.rsqrt(mean + NORM_EPS)
        for c in range(0, width, step):
            xf = x_v[r, c:c + step].astype(F32)
            normed = (xf * inv * gain_v[:, c:c + step]).astype(BF16)
            qi = lax.rem(t + i, n_t)
            n_v[qi // 2, lax.rem(qi, 2), :, c:c + step] = normed
        return inv

    own_k.wait()
    own_v.wait()
    peers = len(offsets) + n_t - 1

    @pl.when(pipe > 0)
    def _():
        pl.semaphore_wait(barrier, peers + 1)

    @pl.when(pipe == 0)
    def _():
        pl.semaphore_wait(barrier, peers)

    own_rows = rows_of(0)
    w_pieces = 4
    prow = blk // w_pieces

    def w_copy(lane, r, q, src, dev):
        cols = pl.ds(pl.multiple_of(src * two, two), two)
        ref = wg_v.at[pl.ds(q * prow, prow), cols]
        return remote(ref, ref, ws_s, ws_r, (r * w_pieces + q) * 2 + lane, dev_t(dev))

    def w_round(r, pieces):
        for q in pieces:
            @pl.when((t - r >= 0) & (t < n_t - 1))
            def _():
                w_copy(0, r, q, t - r, t + 1).start()

            @pl.when((t + r < n_t) & (t > 0))
            def _():
                w_copy(1, r, q, t + r, t - 1).start()

    def w_arrived(r, q):
        @pl.when(t - r - 1 >= 0)
        def _():
            w_copy(0, r, q, t, t).wait_recv()

        @pl.when(t + r + 1 < n_t)
        def _():
            w_copy(1, r, q, t, t).wait_recv()

    def w_sent(r, q):
        @pl.when((t - r >= 0) & (t < n_t - 1))
        def _():
            w_copy(0, r, q, t, t).wait_send()

        @pl.when((t + r < n_t) & (t > 0))
        def _():
            w_copy(1, r, q, t, t).wait_send()

    def w_forward(r):
        for q in range(w_pieces):
            w_arrived(r - 1, q)

            @pl.when((t - r >= 0) & (t < n_t - 1))
            def _():
                w_copy(0, r, q, t - r, t + 1).start()

            @pl.when((t + r < n_t) & (t > 0))
            def _():
                w_copy(1, r, q, t + r, t - 1).start()

    w_round(0, range(w_pieces // 2))

    gain_c.wait()
    x_cs[0].wait()
    inv_v[...] = jnp.broadcast_to(norm_quarter(0), (quarter, 128))
    x_cs[2].wait()
    norm_quarter(2)

    def blk_cols(dd):
        return pl.ds(pl.multiple_of(dd * blk, blk), blk)

    nw = blk // 2

    def part_cols(dd, p):
        return pl.ds(pl.multiple_of(dd * blk + p * nw, nw), nw)

    oth = 1 - hi
    n_sends = []
    for i, (dx, dy) in enumerate(offsets):
        dd = at_xy(dx, dy)
        c = remote(n_v.at[hi, lo, :, blk_cols(dd)], nx_v.at[my, mx, hi], nx_s, nx_r, i, dev_d(dd))
        c.start()
        n_sends.append(c)
    nx_v[my, mx] = n_v[:, lo, :, blk_cols(d)]

    def others(p):
        for i, (dx, dy) in enumerate(offsets):
            dd = at_xy(dx, dy)
            yield remote(
                n_v.at[oth, lo, :, part_cols(dd, p)], nx_v.at[my, mx, oth, :, pl.ds(p * nw, nw)],
                nx_s, nx_r, (p + 1) * len(offsets) + i, dev_d(dd),
            )

    def send_other(p):
        for c in others(p):
            c.start()

    send_other(0)

    for i in (1, 3):
        x_cs[i].wait()
        norm_quarter(i)

    kv = jnp.zeros((seq, two), F32)
    for i in range(n_w):
        w_cs[2 * i].wait()
        w_cs[2 * i + 1].wait()
        kv = kv + jnp.dot(
            n_v[:, :, :, i * wrows:(i + 1) * wrows].reshape(seq, wrows), w_v[i * wrows:(i + 1) * wrows, :],
            preferred_element_type=F32,
        )
    keys = kv[:, :head].astype(BF16)
    values = kv[:, head:].astype(BF16)

    factor = 1.0 / math.sqrt(head)
    seg_c.wait()
    seg_r = jnp.broadcast_to(seg_v[...], (seq, seq))
    ri = lax.broadcasted_iota(jnp.int32, (seq, seq), 0)
    ci = lax.broadcasted_iota(jnp.int32, (seq, seq), 1)
    allowed1 = (ci <= ri) & (seg_r == seg_r.T)
    allowed = jnp.concatenate([allowed1.astype(F32)] * group, axis=0) > 0.5
    q_c.wait()
    oc_c.wait()
    qs = jnp.concatenate([q_v[:, g * head:(g + 1) * head] for g in range(group)], axis=0)
    ocs = jnp.concatenate([oc_v[:, g * head:(g + 1) * head] for g in range(group)], axis=0)
    nt = (((1,), (1,)), ((), ()))
    tn = (((0,), (0,)), ((), ()))
    s = lax.dot_general(qs, keys, nt, preferred_element_type=F32) * factor
    dprob = lax.dot_general(ocs, values, nt, preferred_element_type=F32)
    e = jnp.where(allowed, jnp.exp(s), 0.0)
    probs = e / jnp.sum(e, axis=-1, keepdims=True)
    inner = jnp.sum(probs * dprob, axis=-1, keepdims=True)
    ds_ = (probs * (dprob - inner)).astype(BF16)
    pb = probs.astype(BF16)
    dk = (lax.dot_general(ds_, qs, tn, preferred_element_type=F32) * factor).astype(BF16)
    dv = lax.dot_general(pb, ocs, tn, preferred_element_type=F32).astype(BF16)
    dkv_v[:, :head] = dk
    dkv_v[:, head:] = dv
    msum = jnp.sum(
        dk.astype(F32) * kv[:, :head] + dv.astype(F32) * kv[:, head:], axis=-1, keepdims=True
    )
    mfull = jnp.broadcast_to(msum, (seq, 128))
    mtop = mfull.astype(BF16)
    mlow = (mfull - mtop.astype(F32)).astype(BF16)
    lane = lax.broadcasted_iota(jnp.int32, (seq, 128), 1)
    mp_v[...] = jnp.where(lane < 64, mtop.astype(F32), mlow.astype(F32)).astype(BF16)

    def head_cols(h):
        return pl.ds(pl.multiple_of(h * two + (h // 2) * 128, 128), two)

    def extra_cols(par):
        return pl.ds(pl.multiple_of(par * two, two), two)

    z_sends = []
    for dt in range(1, n_t):
        tt = at_z(dt)
        r = pl.ds(pl.multiple_of(tt * quarter, quarter), quarter)
        c = remote(dkv_v.at[r], ag_v.at[my, mx, :, head_cols(t)], zk_s, zk_r, dt - 1, dev_t(tt))
        c.start()
        z_sends.append(c)
    r = pl.ds(pl.multiple_of(lax.rem(partner + 2, n_t) * quarter, quarter), quarter)
    c = remote(dkv_v.at[r], ax_v.at[my, mx, :, extra_cols(lo)], zk_s, zk_r, n_t - 1, dev_t(partner))
    c.start()
    z_sends.append(c)
    m_sends = []
    for dt in range(1, n_t):
        tt = at_z(dt)
        r = pl.ds(pl.multiple_of(tt * quarter, quarter), quarter)
        c = remote(mp_v.at[r], mr_v.at[dt], zm_s, zm_r, dt - 1, dev_t(tt))
        c.start()
        m_sends.append(c)
    w_round(0, range(w_pieces // 2, w_pieces))
    ag_v[my, mx, :, head_cols(t)] = dkv_v[own_rows, :]
    ax_v[my, mx, :, extra_cols(lo)] = dkv_v[rows_of(2), :]
    mr_v[0] = mp_v[own_rows, :]

    for c in z_sends:
        c.wait()
    for c in m_sends:
        c.wait()

    m = mr_v[0].astype(F32)
    for h in range(1, n_t):
        m = m + mr_v[h].astype(F32)
    m = (m[:, :1] + m[:, 64:65]) * (1.0 / width)
    lane = lax.broadcasted_iota(jnp.int32, (quarter, 128), 1)
    inv_f = inv_v[...]
    both = jnp.where(lane < 64, inv_f, inv_f * m)
    top = both.astype(BF16).astype(F32)
    fine = lax.rem(lane, 64) >= 32
    ag_v[my, mx, :, 2 * two:2 * two + 128] = jnp.where(fine, both - top, top).astype(BF16)

    order = sorted(range(1, side), key=lambda i: -min(i, side - i))
    na = side - 1

    class Gather:
        def __init__(self, buf, ss, rs, cuts):
            self.buf, self.ss, self.rs, self.cuts = buf, ss, rs, cuts

        def piece(self, h, yy, xx):
            return self.buf.at[yy, xx, :, pl.ds(*self.cuts[h])]

        def copy(self, ref, i, axis, n):
            dd = at_xy(i, 0) if axis == 0 else at_xy(0, i)
            return remote(ref, ref, self.ss, self.rs, n, dev_d(dd))

        def first(self, i, h):
            return self.copy(self.piece(h, my, mx), i, h, h * na + i - 1)

        def second(self, i, h, j):
            yy = my if h == 0 else lax.rem(my + side - i, side)
            xx = mx if h == 1 else lax.rem(mx + side - i, side)
            n = 2 * na + (h * side + i) * na + j - 1
            return self.copy(self.piece(h, yy, xx), j, 1 - h, n)

        def begin(self):
            for i in order:
                for h in range(2):
                    self.first(i, h).start()
            self.spread(0, 0)
            self.spread(0, 1)

        def spread(self, i, h):
            for j in order:
                self.second(i, h, j).start()

        def forward(self):
            for i in order:
                for h in range(2):
                    self.first(i, h).wait_recv()
                    self.spread(i, h)

        def finish(self):
            for i in order:
                for h in range(2):
                    self.first(i, h).wait_send()
            for i in range(side):
                for h in range(2):
                    for j in order:
                        self.second(i, h, j).wait()

    cut = 2 * two + 128
    main = Gather(ag_v, a1_s, a1_r, ((0, cut), (cut, 2 * two)))
    extra = Gather(ax_v, a2_s, a2_r, ((0, two), (two, two)))
    main.begin()
    w_forward(1)

    dq = (jnp.dot(ds_, keys, preferred_element_type=F32) * factor).astype(BF16)
    for g in range(group):
        dq_out[:, g * head:(g + 1) * head] = dq[g * seq:(g + 1) * seq, :]

    main.forward()
    w_forward(2)
    for c in n_sends:
        c.wait()
    main.finish()
    @pl.when(pipe < n_pipe - 2)
    def _():
        extra.begin()
        send_other(1)


    for q in range(w_pieces):
        w_arrived(2, q)
    tokens = n_dp * quarter
    row = side * quarter
    gain_b = gain_v[:, blk_cols(d)]
    gain_r = 1.0 / gain_b
    prev = (lax.rem(pipe + n_pipe - 1, n_pipe), d, t)
    dys = (2, 1, 3, 0)

    def chain_copies(j):
        return [remote(sb_v.at[j], sr_v.at[j], c_s, c_r, j, prev)]

    def chain_send(j):
        for c in chain_copies(j):
            c.start()

    def chain_take(j):
        for c in chain_copies(j):
            c.wait_recv()

    def deliver(j):
        dy = dys[j]
        for dx in range(side):
            i = j * side + dx
            if dx or dy:
                deliver_copy(i).start()
            else:
                fr_v[i] = sb_v[j, mx]

    def deliver_copy(i):
        dx, dy = i % side, dys[i // side]
        src = sb_v.at[i // side, lax.rem(mx + dx, side)]
        return remote(src, fr_v.at[i], g_s, g_r, i, dev_d(at_xy(dx, dy)))

    def chain(j):
        chain_take(j)
        tot = cf_v[j] + sr_v[j].reshape(row, blk).astype(F32)
        sb_v[j] = tot.astype(BF16).reshape(side, quarter, blk)

        @pl.when(pipe > 0)
        def _():
            chain_send(j)

    for j, dy in enumerate(dys):
        yy = lax.rem(my + dy, side)
        lhs = ag_v[yy, :, :, :2 * two].reshape(row, 2 * two)
        g = lax.dot_general(lhs, wg_v[:, :2 * two], nt, preferred_element_type=F32)
        lhs = ag_v[yy, :, :, cut:].reshape(row, 2 * two)
        g = g + lax.dot_general(lhs, wg_v[:, 2 * two:], nt, preferred_element_type=F32)
        sc = ag_v[yy, :, :, 2 * two:cut].reshape(row, 128).astype(F32)
        alpha = sc[:, :1] + sc[:, 32:33]
        beta = sc[:, 64:65] + sc[:, 96:97]
        nrm = nx_v[yy, :, hi].reshape(row, blk).astype(F32)
        con = alpha * (gain_b * g) - (beta * nrm) * gain_r
        cf_v[j] = con

        @pl.when(pipe == n_pipe - 1)
        def _():
            sb_v[j] = con.astype(BF16).reshape(side, quarter, blk)
            chain_send(j)

        if j:
            @pl.when(pipe == n_pipe - 2)
            def _():
                chain(j - 1)

    @pl.when(pipe == n_pipe - 2)
    def _():
        chain(side - 1)

    @pl.when(pipe >= n_pipe - 2)
    def _():
        for j in range(side):
            deliver(j)

    @pl.when(pipe >= n_pipe - 2)
    def _():
        extra.begin()
        send_other(1)

    extra.forward()

    for p in range(2):
        for c in others(p):
            c.wait()
    extra.finish()
    nxt_own = nx_v[:, :, hi].reshape(tokens, blk).T
    nxt_oth = nx_v[:, :, oth].reshape(tokens, blk).T
    pair_at = pl.multiple_of(hi * (2 * two + 128), 128)
    own_pair = ag_v[:, :, :, pl.ds(pair_at, 2 * two)]
    part = jnp.dot(nxt_own, own_pair.reshape(tokens, 2 * two), preferred_element_type=F32)
    part = part + jnp.dot(
        nxt_oth, ax_v[...].reshape(tokens, 2 * two), preferred_element_type=F32
    )
    for h in range(2):
        pw_v[h] = part[:, h * two:(h + 1) * two]
    ps_v[...] = pw_v[1 - lo].astype(BF16)

    def chain_sent():
        for j in range(side):
            for c in chain_copies(j):
                c.wait_send()

    @pl.when(pipe >= n_pipe - 2)
    def _():
        chain_sent()

    p_c = remote(ps_v, pr_v, p_s, p_r, 0, dev_t(partner))
    p_c.start()

    @pl.when(pipe < n_pipe - 2)
    def _():
        for j in range(side):
            chain(j)
            deliver(j)

    up_c.wait()

    def finish_block(i):
        dx, dy = i % side, dys[i // side]
        if dx or dy:
            deliver_copy(i).wait_recv()
        cc = blk_cols(at_xy(side - dx, side - dy))
        sc_out[:, cc] = (up_v[:, cc].astype(F32) + fr_v[i].astype(F32)).astype(BF16)

    for i in range(n_dp - side):
        finish_block(i)

    p_c.wait()
    tot = pw_v[lo] + pr_v[...].astype(F32)
    kg_out[...] = tot[:, :head]
    vg_out[...] = tot[:, head:]

    for i in range(n_dp - side, n_dp):
        finish_block(i)

    for i in range(n_dp):
        if i % side or dys[i // side]:
            deliver_copy(i).wait_send()
    for r in range(n_t - 1):
        for q in range(w_pieces):
            w_sent(r, q)

    @pl.when((pipe > 0) & (pipe < n_pipe - 2))
    def _():
        chain_sent()


def write_out(*refs):
    n = 4
    ins, outs, sems = refs[:n], refs[n:2 * n], refs[2 * n]
    stores = [pltpu.make_async_copy(ins[i], outs[i], sems.at[i]) for i in range(n)]
    for o in stores:
        o.start()
    for o in stores:
        o.wait()


def per_device(sizes, section_input, norm_gain, key_weight, value_weight, queries, out_cotangent,
               segment_ids, upstream):
    n_pipe, n_dp, n_t = sizes
    seq, width = section_input.shape[3:]
    head = key_weight.shape[2]
    group = queries.shape[4] // head
    side = math.isqrt(n_dp)
    blk = width // n_dp
    quarter = seq // n_t
    two = 2 * head
    heads = group * head
    dims = (n_pipe, n_dp, n_t, side, seq, width, head, group)
    V = pltpu.VMEM
    DMA = pltpu.SemaphoreType.DMA
    any_spec = pl.BlockSpec(memory_space=pl.ANY)
    noff = n_dp - 1
    nz = n_t - 1
    na = 2 * (side - 1)
    sc, dq, kg, vg = pl.pallas_call(
        functools.partial(kernel, dims),
        out_shape=(
            V((quarter, width), BF16),
            V((seq, heads), BF16),
            V((blk, head), F32),
            V((blk, head), F32),
        ),
        in_specs=[any_spec] * 8,
        out_specs=(pl.BlockSpec(memory_space=V),) * 4,
        scratch_shapes=[
            V((seq, width), BF16),
            V((2, 2, quarter, width), BF16),
            V((width, two), BF16),
            V((blk, n_t * two), BF16),
            V((seq, heads), BF16),
            V((seq, heads), BF16),
            V((1, seq), jnp.int32),
            V((quarter, width), BF16),
            V((1, width), F32),
            V((quarter, 128), F32),
            V((side, side, 2, quarter, blk), BF16),
            V((seq, two), BF16),
            V((seq, 128), BF16),
            V((n_t, quarter, 128), BF16),
            V((side, side, quarter, n_t * two + 128), BF16),
            V((side, side, quarter, 2 * two), BF16),
            V((side, side * quarter, blk), F32),
            V((n_dp, quarter, blk), BF16),
            V((side, side, quarter, blk), BF16),
            V((side, side, quarter, blk), BF16),
            V((2, blk, two), F32),
            V((blk, two), BF16),
            V((blk, two), BF16),
            DMA((19,)),
            DMA((8 * nz,)), DMA((8 * nz,)),
            DMA((3 * noff,)), DMA((3 * noff,)),
            DMA((n_t,)), DMA((n_t,)),
            DMA((nz,)), DMA((nz,)),
            DMA((na + side * na,)), DMA((na + side * na,)),
            DMA((na + side * na,)), DMA((na + side * na,)),
            DMA((n_dp,)), DMA((n_dp,)),
            DMA((n_dp,)), DMA((n_dp,)),
            DMA((1,)), DMA((1,)),
        ],
        compiler_params=pltpu.CompilerParams(
            collective_id=0, has_side_effects=True, vmem_limit_bytes=62 << 20
        ),
        name="attention_backward",
    )(
        section_input.reshape(seq, width),
        norm_gain.reshape(1, width),
        key_weight.reshape(width, head),
        value_weight.reshape(width, head),
        queries.reshape(seq, heads),
        out_cotangent.reshape(seq, heads),
        segment_ids.reshape(1, seq),
        upstream.reshape(quarter, width),
    )
    parts = (sc, dq, kg, vg)
    sc, dq, kg, vg = pl.pallas_call(
        write_out,
        out_shape=tuple(jax.ShapeDtypeStruct(a.shape, a.dtype) for a in parts),
        in_specs=[pl.BlockSpec(memory_space=V)] * 4,
        out_specs=(any_spec,) * 4,
        scratch_shapes=[DMA((4,))],
        compiler_params=pltpu.CompilerParams(vmem_limit_bytes=16 << 20),
        name="write_out",
    )(*parts)
    return (
        sc.reshape(1, 1, 1, quarter, width),
        dq.reshape(1, 1, 1, seq, heads),
        kg[None],
        vg[None],
    )


def solution(mesh):
    sizes = tuple(mesh.shape[a] for a in ("pipe", "dp", "tensor"))
    return jax.shard_map(
        functools.partial(per_device, sizes),
        mesh=mesh,
        in_specs=(
            P("pipe", None, "dp", None, None),
            P("pipe", None),
            P("pipe", None, "tensor"),
            P("pipe", None, "tensor"),
            P("pipe", None, "dp", None, "tensor"),
            P("pipe", None, "dp", None, "tensor"),
            P(None, "dp", None),
            P(None, "dp", "tensor", None),
        ),
        out_specs=(
            P("pipe", None, "dp", "tensor", None),
            P("pipe", None, "dp", None, "tensor"),
            P("pipe", "dp", "tensor"),
            P("pipe", "dp", "tensor"),
        ),
        check_vma=False,
    )
```
